256 devices in a mesh: row: 16 (over y_hi, z), col: 16 (over y_lo, x, core).
Axes of the slice: x: 4, y: 4 (y_hi: 2, y_lo: 2; y = y_hi * 2 + y_lo), z: 8, core: 2. Of those that a mesh axis runs over, the one named last changes fastest.
Arguments:
- tokens: bfloat16 [1024, 8192], P('col', 'row'), may hold values from -6 to 6
- row_order: int32 [1024], P('col'), may hold values from 0 to 1023, as said below
- adapter_id: int32 [1], replicated, may hold values from 0 to 63
- gate_weight: bfloat16 [8192, 28672], P('row', 'col'), may hold values from -0.0625 to 0.0625
- up_weight: bfloat16 [8192, 28672], P('row', 'col'), may hold values from -0.0625 to 0.0625
- down_weight: bfloat16 [28672, 8192], P('col', 'row'), may hold values from -0.03125 to 0.03125
- gate_inner: bfloat16 [64, 8192, 64], P(None, ('row', 'col')), may hold values from -0.0625 to 0.0625
- gate_outer: bfloat16 [64, 64, 28672], P(None, None, ('col', 'row')), may hold values from -0.1796875 to 0.1796875
- up_inner: bfloat16 [64, 8192, 64], P(None, ('row', 'col')), may hold values from -0.0625 to 0.0625
- up_outer: bfloat16 [64, 64, 28672], P(None, None, ('col', 'row')), may hold values from -0.1796875 to 0.1796875
- down_inner: bfloat16 [64, 28672, 64], P(None, ('col', 'row')), may hold values from -0.03125 to 0.03125
- down_outer: bfloat16 [64, 64, 8192], P(None, None, ('row', 'col')), may hold values from -0.1796875 to 0.1796875
Outputs:
- mixed: bfloat16 [1024, 8192], P('col', 'row')
The draws below stay inside these ranges and needn't reach their ends.
Inputs may be any that keep to these rules, and one draw needn't show every extreme that they name: Within each aligned block of 64 rows, row_order holds every index of that same block exactly once.
All inputs are finite; a program needn't handle non-finite values.
Results may differ from the reference program's by a relative error of at most 0.0071.
Values may be sent and summed in bfloat16 or wider, within the bound.
A program may use at most 128 MiB of HBM per device.

```python
import jax
import jax.numpy as jnp

D = 8192
FF = 28672
RANK = 64
POOL = 64
ROWS_COL = 64
ROWS = 1024


def draw_row_order(key, part):
    key = jax.random.fold_in(key, 5)
    blocks = ROWS // ROWS_COL
    keys = jax.random.split(key, blocks)
    shuffled = jax.vmap(lambda one: jax.random.permutation(one, ROWS_COL))(keys)
    offsets = (jnp.arange(blocks, dtype=jnp.int32) * ROWS_COL)[:, None]
    return (shuffled.astype(jnp.int32) + offsets).reshape(ROWS)


def block_scale(rng, extent, pieces, smallest, largest):
    level, own = 1.0, jax.random.fold_in(rng, 6)
    for position, shards_of in pieces:
        heights = jnp.exp(jax.random.uniform(jax.random.fold_in(own, position), (shards_of,), jnp.float32, smallest / len(pieces), largest / len(pieces)))
        level = level * jnp.repeat(heights, extent[position] // shards_of).reshape([-1 if axis == position else 1 for axis in range(len(extent))])
    return level


def gaussian(stream_key, shape, deviation, most, pieces=(), held_as=jnp.bfloat16):
    array = jax.random.normal(stream_key, shape, jnp.float32) * deviation
    if len(pieces) > 0:
        array = block_scale(stream_key, shape, pieces, -0.22, 0.18) * array
    return jnp.clip(array, min=-most, max=most).astype(held_as)


def setup_inputs(seed: int = 0) -> dict:
    splits = jax.random.split(jax.random.key(seed), 13)
    tokens = gaussian(splits[0], (ROWS, D), 1.0, 6.0, ((0, 16), (1, 16)))
    row_order = draw_row_order(jax.random.fold_in(splits[12], 71), 0)
    adapter_id = jax.random.randint(splits[2], (1,), 0, POOL).astype(jnp.int32)
    gate_weight = gaussian(splits[3], (D, FF), D ** -0.5, 0.0625, ((0, 16), (1, 16)))
    up_weight = gaussian(splits[4], (D, FF), D ** -0.5, 0.0625, ((0, 16), (1, 16)))
    down_weight = gaussian(splits[5], (FF, D), FF ** -0.5, 0.03125, ((0, 16), (1, 16)))
    gate_inner = gaussian(splits[6], (POOL, D, RANK), D ** -0.5, 0.0625, ((1, 256),))
    gate_outer = gaussian(splits[7], (POOL, RANK, FF), 0.03, 0.1796875, ((2, 256),))
    up_inner = gaussian(splits[8], (POOL, D, RANK), D ** -0.5, 0.0625, ((1, 256),))
    up_outer = gaussian(splits[9], (POOL, RANK, FF), 0.03, 0.1796875, ((2, 256),))
    down_inner = gaussian(splits[10], (POOL, FF, RANK), FF ** -0.5, 0.03125, ((1, 256),))
    down_outer = gaussian(splits[11], (POOL, RANK, D), 0.03, 0.1796875, ((2, 256),))
    return {"tokens": tokens, "row_order": row_order, "adapter_id": adapter_id, "gate_weight": gate_weight, "up_weight": up_weight, "down_weight": down_weight, "gate_inner": gate_inner, "gate_outer": gate_outer, "up_inner": up_inner, "up_outer": up_outer, "down_inner": down_inner, "down_outer": down_outer}


def merge_one(base, inner, outer, pick):
    low = jnp.dot(inner[pick], outer[pick], preferred_element_type=jnp.float32)
    return (base.astype(jnp.float32) + 2.0 * low).astype(jnp.bfloat16)


def reference(tokens, row_order, adapter_id, gate_weight, up_weight, down_weight, gate_inner, gate_outer, up_inner, up_outer, down_inner, down_outer):
    pick = adapter_id[0]
    merged_gate = merge_one(gate_weight, gate_inner, gate_outer, pick)
    merged_up = merge_one(up_weight, up_inner, up_outer, pick)
    merged_down = merge_one(down_weight, down_inner, down_outer, pick)
    rows = jnp.take(tokens, row_order, axis=0)
    gate = jnp.dot(rows, merged_gate, preferred_element_type=jnp.float32)
    up = jnp.dot(rows, merged_up, preferred_element_type=jnp.float32)
    hidden = (jax.nn.silu(gate) * up).astype(jnp.bfloat16)
    return jnp.dot(hidden, merged_down, preferred_element_type=jnp.float32).astype(jnp.bfloat16)
```

```python
import functools

import jax
import jax.numpy as jnp
from jax import lax
from jax.experimental import pallas as pl
from jax.experimental.pallas import tpu as pltpu
from jax.sharding import PartitionSpec as P

MESH = pl.DeviceIdType.MESH
BF = jnp.bfloat16
F32 = jnp.float32
GROUPS = 7
GW = 256
A_GROUPS = (1, 3, 5, 6)
B_GROUPS = (0, 2, 4)
NA, NB = len(A_GROUPS), len(B_GROUPS)
AGY = (0, 2, 4, 1)
AGZ = (3, 5, 6)
CW, CCW = 0, 1
T00 = (((0,), (0,)), ((), ()))
T11 = (((1,), (1,)), ((), ()))


def dot(a, b, dims=(((1,), (0,)), ((), ()))):
    return lax.dot_general(a, b, dims, preferred_element_type=F32)


def pick_kernel(k_ref, order_ref, tok_ref, gi_ref, ui_ref, di_ref, go_ref, uo_ref, do_ref, rows_ref, inner_ref, outer_ref):
    r = lax.broadcasted_iota(jnp.int32, (64, 128), 0)
    c = lax.broadcasted_iota(jnp.int32, (64, 128), 1)
    left = jnp.where(r == c, 1.0, 0.0).astype(BF)
    right = jnp.where(r + 64 == c, 1.0, 0.0).astype(BF)
    source = lax.broadcasted_iota(jnp.int32, (64, 64), 0)
    one_hot = jnp.where(source == order_ref[...] % 64, 1.0, 0.0).astype(BF)
    rows_ref[...] = dot(one_hot, tok_ref[...], T00).astype(BF).reshape(4, 16, 512)
    inner_ref[0] = (dot(gi_ref[0], left) + dot(ui_ref[0], right)).astype(BF)
    inner_ref[1] = dot(do_ref[0], left, T00).astype(BF)
    outer_ref[0] = (dot(go_ref[0], left, T00) + dot(uo_ref[0], right, T00)).astype(BF)
    outer_ref[1] = dot(di_ref[0], left).astype(BF)


def pick(adapter_id, order, tokens, gi, ui, di, go, uo, do):
    whole = lambda shape: pl.BlockSpec(shape, lambda i, k: (0,) * len(shape))
    chosen = lambda a: pl.BlockSpec((1,) + a.shape[1:], lambda i, k: (k[0], 0, 0))
    return pl.pallas_call(
        pick_kernel,
        out_shape=(
            jax.ShapeDtypeStruct((4, 16, 512), BF),
            jax.ShapeDtypeStruct((2, 32, 128), BF),
            jax.ShapeDtypeStruct((2, 112, 128), BF),
        ),
        grid_spec=pltpu.PrefetchScalarGridSpec(
            num_scalar_prefetch=1,
            grid=(1,),
            in_specs=[whole((1, 64)), whole((64, 512))] + [chosen(a) for a in (gi, ui, di, go, uo, do)],
            out_specs=(whole((4, 16, 512)), whole((2, 32, 128)), whole((2, 112, 128))),
        ),
    )(adapter_id, order.reshape(1, 64), tokens, gi, ui, di, go, uo, do)


def kernel(
    rows_ref, inner_ref, outer_ref, gate_hbm, up_hbm, down_hbm, out_ref,
    wg, wu, wd, x, ibuf, ogu, od, im, part, yrec_a, zrec_a, zrec_b, yrec_b, hid, obuf, orec,
    load_sem, own_sem, x_sem, i_sem, o_sem, gather_send,
    rsz_recv, rsy_recv, agz_recv, agy_recv, ring_send, out_sem,
):
    row, col = lax.axis_index("row"), lax.axis_index("col")
    yh, z = row // 8, row % 8
    chip, core = col // 2, col % 2
    zat = lambda k: (z + k + 8) % 8
    up_dev = (yh * 8 + zat(1), col)
    down_dev = (yh * 8 + zat(-1), col)
    y_dev = ((1 - yh) * 8 + z, col)
    sib_dev = (row, chip * 2 + 1 - core)
    ring_dev = (up_dev, down_dev)

    def remote(src, dst, send, recv, dev):
        return pltpu.make_async_remote_copy(src, dst, send, recv, device_id=dev, device_id_type=MESH)

    def wait_recv(dst, recv):
        remote(dst, dst, gather_send.at[0], recv, y_dev).wait_recv()

    def wait_send(src, send):
        remote(src, src, send, out_sem.at[1], y_dev).wait_send()

    loads = [
        pltpu.make_async_copy(src, dst, load_sem.at[i])
        for i, (src, dst) in enumerate(((gate_hbm, wg), (up_hbm, wu), (down_hbm, wd)))
    ]
    for load in loads:
        load.start()

    barrier = pltpu.get_barrier_semaphore()
    for k in range(1, 16):
        pl.semaphore_signal(barrier, inc=1, device_id=(row, (col + k) % 16), device_id_type=MESH)
    for k in range(1, 8):
        pl.semaphore_signal(barrier, inc=1, device_id=(yh * 8 + zat(k), col), device_id_type=MESH)
    pl.semaphore_signal(barrier, inc=1, device_id=y_dev, device_id_type=MESH)
    pl.semaphore_wait(barrier, 23)

    def o_at(ref, r):
        return ref.at[pl.ds(pl.multiple_of(r * 112, 16), 112)]

    def x_at(chip_, core_):
        return x.at[pl.ds(core_ * 4, 4), pl.ds(pl.multiple_of(chip_ * 16, 16), 16)]

    own = []

    def keep(src, dst, i):
        copy = pltpu.make_async_copy(src, dst, own_sem.at[i])
        copy.start()
        own.append(copy)

    order = (1, 7, 2, 6, 3, 5, 4)
    for n, ref in ((0, ogu), (1, od)):
        src = outer_ref.at[n]
        keep(src, o_at(ref, row), n)
        if n == 0:
            for k in order:
                remote(src, o_at(ref, row), gather_send.at[2 + n], o_sem.at[n, 0, k], (yh * 8 + zat(k), col)).start()
            remote(src, o_at(ref, row), gather_send.at[2 + n], o_sem.at[n, 1, 0], y_dev).start()
            keep(inner_ref, ibuf.at[col], 2)
            for k in order:
                remote(inner_ref, ibuf.at[col], gather_send.at[1], i_sem.at[0, k], (row, (chip + k) % 8 * 2 + core)).start()
            remote(inner_ref, ibuf.at[col], gather_send.at[1], i_sem.at[1, 0], sib_dev).start()
            keep(rows_ref, x_at(chip, core), 3)
            for k in order:
                remote(rows_ref, x_at(chip, core), gather_send.at[0], x_sem.at[0, k], (row, (chip + k) % 8 * 2 + core)).start()
            remote(rows_ref, x_at(chip, core), gather_send.at[0], x_sem.at[1, 0], sib_dev).start()
        else:
            for k in order:
                remote(src, o_at(ref, row), gather_send.at[2 + n], o_sem.at[n, 0, k], (yh * 8 + zat(k), col)).start()
            remote(src, o_at(ref, row), gather_send.at[2 + n], o_sem.at[n, 1, 0], y_dev).start()

    def pass_outer(n, ref):
        for k in order:
            here = o_at(ref, yh * 8 + zat(-k))
            wait_recv(here, o_sem.at[n, 0, k])
            remote(here, here, gather_send.at[2 + n], o_sem.at[n, 1, k], y_dev).start()

    def end_outer(n, ref):
        for k in range(8):
            wait_recv(o_at(ref, (1 - yh) * 8 + zat(-k)), o_sem.at[n, 1, k])

    for k in order:
        here = ibuf.at[(chip + 8 - k) % 8 * 2 + core]
        wait_recv(here, i_sem.at[0, k])
        remote(here, here, gather_send.at[1], i_sem.at[1, k], sib_dev).start()
    pass_outer(0, ogu)
    for k in order:
        here = x_at((chip + 8 - k) % 8, core)
        wait_recv(here, x_sem.at[0, k])
        remote(here, here, gather_send.at[0], x_sem.at[1, k], sib_dev).start()
    for copy in own:
        copy.wait()
    for k in range(8):
        wait_recv(ibuf.at[(chip + 8 - k) % 8 * 2 + 1 - core], i_sem.at[1, k])
    lane = lax.broadcasted_iota(jnp.int32, (512, 128), 1)
    pairs = ibuf[:, 0].reshape(512, 128)
    im[0] = jnp.where(lane < 64, pairs, jnp.zeros_like(pairs))
    im[1] = jnp.where(lane >= 64, pairs, jnp.zeros_like(pairs))
    im[2] = ibuf[:, 1].reshape(512, 128)
    end_outer(0, ogu)
    loads[0].wait()
    loads[1].wait()

    def merge(g):
        factor = ogu[g * GW:(g + 1) * GW]
        for half, w in enumerate((wg, wu)):
            low = dot(im[half], factor, T11)
            cols = slice(g * GW, (g + 1) * GW)
            w[:, cols] = (w[:, cols].astype(F32) + 2.0 * low).astype(BF)

    def merge_down():
        @pl.loop(0, 7)
        def _(i):
            at = pl.ds(pl.multiple_of(i * 256, 256), 256)
            low = dot(od[at], im[2], T11)
            wd[at] = (wd[at].astype(F32) + 2.0 * low).astype(BF)

    def products(g):
        cols = slice(g * GW, (g + 1) * GW)

        @pl.loop(0, 2)
        def _(i):
            rows = x[pl.ds(i * 4, 4)].reshape(512, 512)
            for half, w in enumerate((wg, wu)):
                term = dot(rows, w[:, cols])
                part[g, pl.ds(i * 4, 4), :, :, half * GW:(half + 1) * GW] = term.astype(BF).reshape(4, 2, 64, GW)

    def rs_refs(g):
        if g in A_GROUPS:
            n = A_GROUPS.index(g)
            return zrec_a.at[n], (lambda d: part.at[g, d, yh]), yrec_a.at[n]
        n = B_GROUPS.index(g)
        return zrec_b.at[n], (lambda d: part.at[g, d]), None

    def lanes(half):
        return pl.ds(half * GW, GW)

    def rs_y(g):
        _, _, yrec = rs_refs(g)
        remote(part.at[g, :, 1 - yh], yrec, ring_send.at[1, g], rsy_recv.at[g], y_dev).start()

    def rs_1(g):
        zrec, at, yrec = rs_refs(g)
        d = zat(4)
        if yrec is not None:
            wait_recv(yrec, rsy_recv.at[g])
            at(d)[...] = (at(d)[...].astype(F32) + yrec[d].astype(F32)).astype(BF)
        for way in (CW, CCW):
            remote(
                at(d).at[..., lanes(way)], zrec.at[way, 0].at[..., lanes(way)],
                ring_send.at[0, g], rsz_recv.at[g, way, 0], ring_dev[way],
            ).start()

    def rs_s(g, s):
        zrec, at, yrec = rs_refs(g)
        for way in (CW, CCW):
            d = zat(5 - s if way == CW else s - 5)
            got = zrec.at[way, s - 2]
            spot = at(d)
            if s == 2:
                wait_recv(got.at[..., lanes(way)], rsz_recv.at[g, way, 0])
                for half in (0, 1):
                    total = spot[..., lanes(half)].astype(F32)
                    if yrec is not None:
                        total = total + yrec[d, :, lanes(half)].astype(F32)
                    if half == way:
                        total = total + got[..., lanes(half)].astype(F32)
                    if half == way or yrec is not None:
                        spot[..., lanes(half)] = total.astype(BF)
            else:
                wait_recv(got, rsz_recv.at[g, way, s - 2])
                total = spot[...].astype(F32) + got[...].astype(F32)
                if yrec is not None:
                    total = total + yrec[d].astype(F32)
                spot[...] = total.astype(BF)
            remote(spot, zrec.at[way, s - 1], ring_send.at[0, g], rsz_recv.at[g, way, s - 1], ring_dev[way]).start()

    def rs_end(g):
        zrec, at, _ = rs_refs(g)
        for way in (CW, CCW):
            wait_recv(zrec.at[way, 3], rsz_recv.at[g, way, 3])

    def rs_pass(g):
        rs_end(g)
        zrec, at, _ = rs_refs(g)
        away = part.at[g, z, 1 - yh]
        total = away[...].astype(F32) + zrec[CW, 3, 1 - yh].astype(F32) + zrec[CCW, 3, 1 - yh].astype(F32)
        away[...] = total.astype(BF)
        remote(away, yrec_b.at[B_GROUPS.index(g)], ring_send.at[1, g], rsy_recv.at[g], y_dev).start()

    def hidden(g):
        if g in A_GROUPS:
            rs_end(g)
            zrec, at, yrec = rs_refs(g)
            terms = (part.at[g, z, yh], yrec.at[z], zrec.at[CW, 3], zrec.at[CCW, 3])
        else:
            n = B_GROUPS.index(g)
            wait_recv(yrec_b.at[n], rsy_recv.at[g])
            terms = (part.at[g, z, yh], zrec_b.at[n, CW, 3, yh], zrec_b.at[n, CCW, 3, yh], yrec_b.at[n])
        sums = []
        for half in (0, 1):
            total = terms[0][:, lanes(half)].astype(F32)
            for term in terms[1:]:
                total = total + term[:, lanes(half)].astype(F32)
            sums.append(total)
        gate, up = sums
        hid[z, yh, :, g * GW:(g + 1) * GW] = (gate / (1.0 + jnp.exp(-gate)) * up).astype(BF)

    def h_at(g, d, s=1, way=None):
        lo, n = (g * GW, GW) if s < 4 else (g * GW + way * GW // 2, GW // 2)
        if g in AGY:
            return hid.at[d, yh, :, pl.ds(lo, n)]
        return hid.at[d, :, :, pl.ds(lo, n)]

    def ag_y(g, d):
        ref = hid.at[d, yh, :, pl.ds(g * GW, GW)]
        remote(ref, ref, ring_send.at[3, g], agy_recv.at[g], y_dev).start()

    def ag_1(g):
        if g in AGY:
            ag_y(g, z)
        else:
            wait_recv(hid.at[z, 1 - yh, :, pl.ds(g * GW, GW)], agy_recv.at[g])
        for way in (CW, CCW):
            ref = h_at(g, z)
            remote(ref, ref, ring_send.at[2, g], agz_recv.at[g, way, 0], ring_dev[way]).start()

    def ag_s(g, s):
        for way in (CW, CCW):
            d = zat(1 - s if way == CW else s - 1)
            wait_recv(h_at(g, d), agz_recv.at[g, way, s - 2])
            ref = h_at(g, d, s, way)
            remote(ref, ref, ring_send.at[2, g], agz_recv.at[g, way, s - 1], ring_dev[way]).start()
            if g in AGY:
                ag_y(g, d)

    def ag_end(g):
        for way in (CW, CCW):
            wait_recv(h_at(g, zat(4), 4, way), agz_recv.at[g, way, 3])
        if g in AGY:
            ag_y(g, zat(4))

    def ag_fin(g):
        wait_recv(hid.at[:, 1 - yh, :, pl.ds(g * GW, GW)], agy_recv.at[g])

    def down(d):
        term = dot(hid[d].reshape(128, GROUPS * GW), wd[...])
        obuf[d] = term.astype(BF).reshape(8, 16, 512)

        @pl.loop(0, 8)
        def _(j):
            to = j * 2 + d // 4

            @pl.when(to != col)
            def _():
                remote(
                    obuf.at[d, j], orec.at[(to + 15 - col) % 16, d % 4],
                    out_sem.at[0], out_sem.at[1], (row, to),
                ).start()

    def start(g):
        merge(g)
        products(g)
        if g in A_GROUPS:
            rs_y(g)
        else:
            rs_1(g)

    for k in range(8):
        wait_recv(x_at((chip + 8 - k) % 8, 1 - core), x_sem.at[1, k])

    b0, b1, b2 = B_GROUPS
    a0, a1, a2, a3 = A_GROUPS
    start(b0)
    start(a0)
    start(b1)
    start(b2)
    rs_s(b0, 2)
    start(a1)
    rs_s(b1, 2)
    start(a2)
    rs_s(b2, 2)
    start(a3)
    pass_outer(1, od)
    for g in B_GROUPS:
        rs_s(g, 3)
    rs_1(a0)
    end_outer(1, od)
    loads[2].wait()
    merge_down()
    for g in B_GROUPS:
        rs_s(g, 4)
    rs_s(a0, 2)
    rs_1(a1)
    for g in B_GROUPS:
        rs_pass(g)
    rs_s(a0, 3)
    rs_s(a1, 2)
    rs_s(a0, 4)
    rs_s(a1, 3)
    for g in B_GROUPS:
        hidden(g)
        ag_1(g)
    rs_s(a1, 4)
    rs_1(a2)
    for g in B_GROUPS:
        ag_s(g, 2)
    hidden(a0)
    ag_1(a0)
    rs_s(a2, 2)
    hidden(a1)
    remote_own(hid, a1, z, yh, agy_recv, ring_send, remote, y_dev)
    for g in B_GROUPS:
        ag_s(g, 3)
    ag_s(a0, 2)
    rs_1(a3)
    rs_s(a2, 3)
    for g in B_GROUPS:
        ag_s(g, 4)
    rs_s(a3, 2)
    ag_s(a0, 3)
    ag_1(a1)
    rs_s(a2, 4)
    rs_s(a3, 3)
    for g in B_GROUPS:
        ag_end(g)
    ag_s(a0, 4)
    ag_s(a1, 2)
    rs_s(a3, 4)
    hidden(a2)
    remote_own(hid, a2, z, yh, agy_recv, ring_send, remote, y_dev)
    ag_end(a0)
    ag_s(a1, 3)
    hidden(a3)
    remote_own(hid, a3, z, yh, agy_recv, ring_send, remote, y_dev)
    ag_1(a2)
    ag_s(a1, 4)
    ag_1(a3)
    for g in AGY:
        ag_fin(g)
    ag_s(a2, 2)
    ag_s(a3, 2)
    ag_end(a1)
    down(z)
    down(zat(1))
    down(zat(-1))
    ag_s(a2, 3)
    ag_s(a3, 3)
    down(zat(2))
    down(zat(-2))
    ag_s(a2, 4)
    ag_s(a3, 4)
    down(zat(3))
    down(zat(-3))
    ag_end(a2)
    ag_end(a3)
    down(zat(4))

    wait_recv(orec, out_sem.at[1])
    for p in range(4):
        total = obuf[core * 4 + p, chip].astype(F32)
        for k in range(15):
            total = total + orec[k, p].astype(F32)
        out_ref[p] = total.astype(BF)

    wait_send(orec, out_sem.at[0])
    wait_send(orec, gather_send.at[0])
    wait_send(ibuf.at[pl.ds(0, 15)], gather_send.at[1])
    wait_send(ogu.at[pl.ds(0, 15 * 112)], gather_send.at[2])
    wait_send(od.at[pl.ds(0, 15 * 112)], gather_send.at[3])
    for g in range(GROUPS):
        cols = pl.ds(g * GW, GW)
        if g in A_GROUPS:
            wait_send(part.at[g, pl.ds(0, 7), 0], ring_send.at[0, g])
            wait_send(part.at[g, :, 0], ring_send.at[1, g])
        else:
            wait_send(part.at[g, pl.ds(0, 7)], ring_send.at[0, g])
            wait_send(part.at[g, 0, 0], ring_send.at[1, g])
        if g in AGY:
            wait_send(hid.at[pl.ds(0, 7), 0, :, cols], ring_send.at[2, g])
            wait_send(hid.at[:, 0, :, cols], ring_send.at[3, g])
        else:
            wait_send(hid.at[pl.ds(0, 7), :, :, cols], ring_send.at[2, g])
            wait_send(hid.at[0, 0, :, cols], ring_send.at[3, g])


def remote_own(hid, g, z, yh, agy_recv, ring_send, remote, y_dev):
    ref = hid.at[z, yh, :, pl.ds(g * GW, GW)]
    remote(ref, ref, ring_send.at[3, g], agy_recv.at[g], y_dev).start()


def layer(rows, inner, outer, gate_weight, up_weight, down_weight):
    vmem = pl.BlockSpec(memory_space=pltpu.VMEM)
    hbm = pl.BlockSpec(memory_space=pl.ANY)
    dma = pltpu.SemaphoreType.DMA
    return pl.pallas_call(
        kernel,
        out_shape=jax.ShapeDtypeStruct((4, 16, 512), BF),
        in_specs=[vmem, vmem, vmem, hbm, hbm, hbm],
        out_specs=vmem,
        scratch_shapes=[
            pltpu.VMEM((512, 1792), BF),
            pltpu.VMEM((512, 1792), BF),
            pltpu.VMEM((1792, 512), BF),
            pltpu.VMEM((8, 128, 512), BF),
            pltpu.VMEM((16, 2, 32, 128), BF),
            pltpu.VMEM((1792, 128), BF),
            pltpu.VMEM((1792, 128), BF),
            pltpu.VMEM((3, 512, 128), BF),
            pltpu.VMEM((GROUPS, 8, 2, 64, 2 * GW), BF),
            pltpu.VMEM((NA, 8, 64, 2 * GW), BF),
            pltpu.VMEM((NA, 2, 4, 64, 2 * GW), BF),
            pltpu.VMEM((NB, 2, 4, 2, 64, 2 * GW), BF),
            pltpu.VMEM((NB, 64, 2 * GW), BF),
            pltpu.VMEM((8, 2, 64, GROUPS * GW), BF),
            pltpu.VMEM((8, 8, 16, 512), BF),
            pltpu.VMEM((15, 4, 16, 512), BF),
            dma((3,)),
            dma((4,)),
            dma((2, 8)),
            dma((2, 8)),
            dma((2, 2, 8)),
            dma((4,)),
            dma((GROUPS, 2, 4)),
            dma((GROUPS,)),
            dma((GROUPS, 2, 4)),
            dma((GROUPS,)),
            dma((4, GROUPS)),
            dma((2,)),
        ],
        compiler_params=pltpu.CompilerParams(
            collective_id=0, has_side_effects=True, vmem_limit_bytes=56 * 2**20
        ),
    )(rows, inner, outer, gate_weight, up_weight, down_weight)


def body(
    tokens, row_order, adapter_id, gate_weight, up_weight, down_weight,
    gate_inner, gate_outer, up_inner, up_outer, down_inner, down_outer,
):
    rows, inner, outer = pick(
        adapter_id, row_order, tokens, gate_inner, up_inner, down_inner, gate_outer, up_outer, down_outer
    )
    return layer(rows, inner, outer, gate_weight, up_weight, down_weight).reshape(64, 512)


def solution(mesh):
    return jax.shard_map(
        body,
        mesh=mesh,
        in_specs=(
            P("col", "row"),
            P("col"),
            P(),
            P("row", "col"),
            P("row", "col"),
            P("col", "row"),
            P(None, ("row", "col"), None),
            P(None, None, ("col", "row")),
            P(None, ("row", "col"), None),
            P(None, None, ("col", "row")),
            P(None, ("col", "row"), None),
            P(None, None, ("row", "col")),
        ),
        out_specs=P("col", "row"),
        check_vma=False,
    )
```

```python
import functools

import jax
import jax.numpy as jnp
from jax import lax
from jax.experimental import pallas as pl
from jax.experimental.pallas import tpu as pltpu
from jax.sharding import PartitionSpec as P

MESH = pl.DeviceIdType.MESH
BF = jnp.bfloat16
F32 = jnp.float32
GROUPS = 7
GW = 256
A_GROUPS = (1, 3, 5)
B_GROUPS = (0, 2, 4, 6)
NA, NB = len(A_GROUPS), len(B_GROUPS)
AGY = (0, 2, 4, 6)
AGZ = (1, 3, 5)
CW, CCW = 0, 1
ORDER = (
    ("start", 0), ("start", 4), ("start", 2), ("start", 6), ("rs", 0, 2), ("start", 3), ("od",), ("rs", 4, 2),
    ("rs", 2, 2), ("rs", 6, 2), ("start", 1), ("mdown",), ("rs", 0, 3), ("rs", 4, 3), ("rs", 3, 1), ("start", 5),
    ("rs", 2, 3), ("rs", 6, 3), ("rs", 0, 4), ("rs", 1, 1), ("rs", 4, 4), ("rs", 3, 2), ("rs", 2, 4), ("rs", 6, 4),
    ("rs", 5, 1), ("pass", 0), ("rs", 1, 2), ("pass", 4), ("rs", 3, 3), ("pass", 2), ("pass", 6), ("hid", 0),
    ("rs", 5, 2), ("hid", 4), ("rs", 1, 3), ("hid", 2), ("rs", 3, 4), ("ag", 0, 2), ("hid", 6), ("rs", 5, 3),
    ("ag", 4, 2), ("rs", 1, 4), ("ag", 2, 2), ("hid", 3), ("ag", 0, 3), ("ag", 6, 2), ("rs", 5, 4), ("ag", 3, 1),
    ("ag", 4, 3), ("hid", 1), ("ag", 2, 3), ("ag", 0, 4), ("ag", 6, 3), ("hid", 5), ("ag", 1, 1), ("ag", 3, 2),
    ("ag", 4, 4), ("ag", 2, 4), ("ag", 0, 5), ("ag", 6, 4), ("ag", 5, 1), ("ag", 1, 2), ("ag", 3, 3), ("ag", 4, 5),
    ("ag", 2, 5), ("ag", 6, 5), ("fin", 0), ("ag", 5, 2), ("ag", 1, 3), ("fin", 4), ("fin", 2), ("ag", 3, 4),
    ("fin", 6), ("down", 0), ("ag", 5, 3), ("down", 1), ("ag", 3, 5), ("ag", 1, 4), ("down", 2), ("ag", 5, 4),
    ("down", 3), ("ag", 1, 5), ("ag", 5, 5), ("down", 4),
)
T00 = (((0,), (0,)), ((), ()))
T11 = (((1,), (1,)), ((), ()))


def dot(a, b, dims=(((1,), (0,)), ((), ()))):
    return lax.dot_general(a, b, dims, preferred_element_type=F32)


def kernel(
    pick_ref, order_ref, tokens_ref, gi_hbm, ui_hbm, di_hbm, go_hbm, uo_hbm, do_hbm, gate_hbm, up_hbm, down_hbm, out_ref,
    gi, ui, di, go, uo, do,
    wg, wu, wd, x, ibuf, ogu, od, im, part, yrec_a, zrec_a, zrec_b, yrec_b, hid, obuf, orec,
    load_sem, x_sem, i_sem, o_sem, gather_send,
    rsz_recv, rsy_recv, agz_recv, agy_recv, ring_send, out_sem,
):
    row, col = lax.axis_index("row"), lax.axis_index("col")
    yh, z = row // 8, row % 8
    chip, core = col // 2, col % 2
    zat = lambda k: (z + k + 8) % 8
    up_dev = (yh * 8 + zat(1), col)
    down_dev = (yh * 8 + zat(-1), col)
    y_dev = ((1 - yh) * 8 + z, col)
    sib_dev = (row, chip * 2 + 1 - core)
    ring_dev = (up_dev, down_dev)

    def remote(src, dst, send, recv, dev):
        return pltpu.make_async_remote_copy(src, dst, send, recv, device_id=dev, device_id_type=MESH)

    def wait_recv(dst, recv):
        remote(dst, dst, gather_send.at[0], recv, y_dev).wait_recv()

    def wait_send(src, send):
        remote(src, src, send, out_sem.at[1], y_dev).wait_send()

    pools = ((go_hbm, go), (uo_hbm, uo), (gi_hbm, gi), (ui_hbm, ui), (di_hbm, di), (do_hbm, do))
    weights = ((gate_hbm, wg), (up_hbm, wu), (down_hbm, wd))
    loads = [pltpu.make_async_copy(src, dst, load_sem.at[i]) for i, (src, dst) in enumerate(pools + weights)]
    for load in loads:
        load.start()

    barrier = pltpu.get_barrier_semaphore()
    for k in range(1, 16):
        pl.semaphore_signal(barrier, inc=1, device_id=(row, (col + k) % 16), device_id_type=MESH)
    for k in range(1, 8):
        pl.semaphore_signal(barrier, inc=1, device_id=(yh * 8 + zat(k), col), device_id_type=MESH)
    pl.semaphore_signal(barrier, inc=1, device_id=y_dev, device_id_type=MESH)

    def o_at(ref, r):
        return ref.at[pl.ds(pl.multiple_of(r * 112, 16), 112)]

    def x_at(chip_, core_):
        return x.at[pl.ds(core_ * 4, 4), pl.ds(pl.multiple_of(chip_ * 16, 16), 16)]

    k = pick_ref[0]
    r128 = lax.broadcasted_iota(jnp.int32, (64, 128), 0)
    c128 = lax.broadcasted_iota(jnp.int32, (64, 128), 1)
    left = jnp.where(r128 == c128, 1.0, 0.0).astype(BF)
    right = jnp.where(r128 + 64 == c128, 1.0, 0.0).astype(BF)
    one_hot = jnp.where(lax.broadcasted_iota(jnp.int32, (64, 64), 0) == order_ref[...] % 64, 1.0, 0.0).astype(BF)
    x_at(chip, core)[...] = dot(one_hot, tokens_ref[...], T00).astype(BF).reshape(4, 16, 512)
    loads[0].wait()
    loads[1].wait()
    o_at(ogu, row)[...] = (dot(go[k], left, T00) + dot(uo[k], right, T00)).astype(BF)
    loads[2].wait()
    loads[3].wait()
    ibuf[col, 0] = (dot(gi[k], left) + dot(ui[k], right)).astype(BF)
    loads[4].wait()
    loads[5].wait()
    ibuf[col, 1] = dot(do[k], left).astype(BF)
    o_at(od, row)[...] = dot(di[k], left, T00).astype(BF)
    pl.semaphore_wait(barrier, 23)

    far = (4, 3, 5, 2, 6, 1, 7)
    near = (1, 7, 2, 6, 3, 5, 4)

    def z_send(n, ref):
        here = o_at(ref, row)
        for k in far:
            remote(here, here, gather_send.at[2 + n], o_sem.at[n, 0, k], (yh * 8 + zat(k), col)).start()
        remote(here, here, gather_send.at[2 + n], o_sem.at[n, 1, 0], y_dev).start()

    def col_send(here, n, sem):
        for k in near:
            remote(here, here, gather_send.at[n], sem.at[0, k], (row, (chip + k) % 8 * 2 + core)).start()
        remote(here, here, gather_send.at[n], sem.at[1, 0], sib_dev).start()

    def z_pass(n, ref):
        for k in near:
            here = o_at(ref, yh * 8 + zat(-k))
            wait_recv(here, o_sem.at[n, 0, k])
            remote(here, here, gather_send.at[2 + n], o_sem.at[n, 1, k], y_dev).start()

    def z_end(n, ref):
        for k in range(8):
            wait_recv(o_at(ref, (1 - yh) * 8 + zat(-k)), o_sem.at[n, 1, k])

    def col_pass(at, n, sem):
        for k in near:
            here = at((chip + 8 - k) % 8, core)
            wait_recv(here, sem.at[0, k])
            remote(here, here, gather_send.at[n], sem.at[1, k], sib_dev).start()

    def col_end(at, n, sem):
        for k in range(8):
            wait_recv(at((chip + 8 - k) % 8, 1 - core), sem.at[1, k])

    i_at = lambda chip_, core_: ibuf.at[chip_ * 2 + core_]
    z_send(0, ogu)
    col_send(i_at(chip, core), 1, i_sem)
    col_send(x_at(chip, core), 0, x_sem)
    z_send(1, od)
    col_pass(i_at, 1, i_sem)
    z_pass(0, ogu)
    col_pass(x_at, 0, x_sem)
    col_end(i_at, 1, i_sem)
    lane = lax.broadcasted_iota(jnp.int32, (512, 128), 1)
    pairs = ibuf[:, 0].reshape(512, 128)
    im[0] = jnp.where(lane < 64, pairs, jnp.zeros_like(pairs))
    im[1] = jnp.where(lane >= 64, pairs, jnp.zeros_like(pairs))
    im[2] = ibuf[:, 1].reshape(512, 128)
    loads[6].wait()
    loads[7].wait()
    z_end(0, ogu)
    col_end(x_at, 0, x_sem)

    def merge(g):
        factor = ogu[g * GW:(g + 1) * GW]
        for half, w in enumerate((wg, wu)):
            low = dot(im[half], factor, T11)
            cols = slice(g * GW, (g + 1) * GW)
            w[:, cols] = (w[:, cols].astype(F32) + 2.0 * low).astype(BF)

    def merge_down():
        z_end(1, od)
        loads[8].wait()

        @pl.loop(0, 7)
        def _(i):
            at = pl.ds(pl.multiple_of(i * 256, 256), 256)
            low = dot(od[at], im[2], T11)
            wd[at] = (wd[at].astype(F32) + 2.0 * low).astype(BF)

    def products(g):
        cols = slice(g * GW, (g + 1) * GW)

        @pl.loop(0, 2)
        def _(i):
            rows = x[pl.ds(i * 4, 4)].reshape(512, 512)
            for half, w in enumerate((wg, wu)):
                term = dot(rows, w[:, cols])
                part[g, pl.ds(i * 4, 4), :, :, half * GW:(half + 1) * GW] = term.astype(BF).reshape(4, 2, 64, GW)

    def rs_refs(g):
        if g in A_GROUPS:
            n = A_GROUPS.index(g)
            return zrec_a.at[n], (lambda d: part.at[g, d, yh]), yrec_a.at[n]
        n = B_GROUPS.index(g)
        return zrec_b.at[n], (lambda d: part.at[g, d]), None

    def lanes(half):
        return pl.ds(half * GW, GW)

    def rs_y(g):
        _, _, yrec = rs_refs(g)
        for k in (4, 3, 5, 2, 6, 1, 7, 0):
            d = zat(k)
            remote(part.at[g, d, 1 - yh], yrec.at[d], ring_send.at[1, g], rsy_recv.at[g, k], y_dev).start()

    def y_wait(g, k):
        _, _, yrec = rs_refs(g)
        wait_recv(yrec.at[zat(k)], rsy_recv.at[g, k])

    def rs_1(g):
        zrec, at, yrec = rs_refs(g)
        d = zat(4)
        if yrec is not None:
            y_wait(g, 4)
            at(d)[...] = (at(d)[...].astype(F32) + yrec[d].astype(F32)).astype(BF)
        for way in (CW, CCW):
            remote(
                at(d).at[..., lanes(way)], zrec.at[way, 0].at[..., lanes(way)],
                ring_send.at[0, g], rsz_recv.at[g, way, 0], ring_dev[way],
            ).start()

    def rs_s(g, s):
        zrec, at, yrec = rs_refs(g)
        for way in (CW, CCW):
            d = zat(5 - s if way == CW else s - 5)
            if yrec is not None:
                y_wait(g, 5 - s if way == CW else s + 3)
            got = zrec.at[way, s - 2]
            spot = at(d)
            if s == 2:
                wait_recv(got.at[..., lanes(way)], rsz_recv.at[g, way, 0])
                for half in (0, 1):
                    total = spot[..., lanes(half)].astype(F32)
                    if yrec is not None:
                        total = total + yrec[d, :, lanes(half)].astype(F32)
                    if half == way:
                        total = total + got[..., lanes(half)].astype(F32)
                    if half == way or yrec is not None:
                        spot[..., lanes(half)] = total.astype(BF)
            else:
                wait_recv(got, rsz_recv.at[g, way, s - 2])
                total = spot[...].astype(F32) + got[...].astype(F32)
                if yrec is not None:
                    total = total + yrec[d].astype(F32)
                spot[...] = total.astype(BF)
            remote(spot, zrec.at[way, s - 1], ring_send.at[0, g], rsz_recv.at[g, way, s - 1], ring_dev[way]).start()

    def rs_end(g):
        zrec, at, _ = rs_refs(g)
        for way in (CW, CCW):
            wait_recv(zrec.at[way, 3], rsz_recv.at[g, way, 3])

    def rs_pass(g):
        rs_end(g)
        zrec, at, _ = rs_refs(g)
        away = part.at[g, z, 1 - yh]
        total = away[...].astype(F32) + zrec[CW, 3, 1 - yh].astype(F32) + zrec[CCW, 3, 1 - yh].astype(F32)
        away[...] = total.astype(BF)
        remote(away, yrec_b.at[B_GROUPS.index(g)], ring_send.at[1, g], rsy_recv.at[g, 0], y_dev).start()

    def hidden(g):
        if g in A_GROUPS:
            rs_end(g)
            y_wait(g, 0)
            zrec, at, yrec = rs_refs(g)
            terms = (part.at[g, z, yh], yrec.at[z], zrec.at[CW, 3], zrec.at[CCW, 3])
        else:
            n = B_GROUPS.index(g)
            wait_recv(yrec_b.at[n], rsy_recv.at[g, 0])
            terms = (part.at[g, z, yh], zrec_b.at[n, CW, 3, yh], zrec_b.at[n, CCW, 3, yh], yrec_b.at[n])
        sums = []
        for half in (0, 1):
            total = terms[0][:, lanes(half)].astype(F32)
            for term in terms[1:]:
                total = total + term[:, lanes(half)].astype(F32)
            sums.append(total)
        gate, up = sums
        hid[z, yh, :, g * GW:(g + 1) * GW] = (gate / (1.0 + jnp.exp(-gate)) * up).astype(BF)
        ag_y(g, z)
        if g in AGY:
            ag_z(g)

    def h_at(g, d, s=1, way=None):
        lo, n = (g * GW, GW) if s < 4 else (g * GW + way * GW // 2, GW // 2)
        if g in AGY:
            return hid.at[d, yh, :, pl.ds(lo, n)]
        return hid.at[d, :, :, pl.ds(lo, n)]

    def ag_y(g, d):
        ref = hid.at[d, yh, :, pl.ds(g * GW, GW)]
        remote(ref, ref, ring_send.at[3, g], agy_recv.at[g], y_dev).start()

    def ag_z(g):
        for way in (CW, CCW):
            ref = h_at(g, z)
            remote(ref, ref, ring_send.at[2, g], agz_recv.at[g, way, 0], ring_dev[way]).start()

    def ag_1(g):
        wait_recv(hid.at[z, 1 - yh, :, pl.ds(g * GW, GW)], agy_recv.at[g])
        ag_z(g)

    def ag_s(g, s):
        for way in (CW, CCW):
            d = zat(1 - s if way == CW else s - 1)
            wait_recv(h_at(g, d), agz_recv.at[g, way, s - 2])
            ref = h_at(g, d, s, way)
            remote(ref, ref, ring_send.at[2, g], agz_recv.at[g, way, s - 1], ring_dev[way]).start()
            if g in AGY:
                ag_y(g, d)

    def ag_end(g):
        for way in (CW, CCW):
            wait_recv(h_at(g, zat(4), 4, way), agz_recv.at[g, way, 3])
        if g in AGY:
            ag_y(g, zat(4))

    def ag_fin(g):
        wait_recv(hid.at[:, 1 - yh, :, pl.ds(g * GW, GW)], agy_recv.at[g])

    def down(d):
        term = dot(hid[d].reshape(128, GROUPS * GW), wd[...])
        obuf[d] = term.astype(BF).reshape(8, 16, 512)

        @pl.loop(0, 8)
        def _(j):
            to = j * 2 + d // 4

            @pl.when(to != col)
            def _():
                remote(
                    obuf.at[d, j], orec.at[(to + 15 - col) % 16, d % 4],
                    out_sem.at[0], out_sem.at[1], (row, to),
                ).start()

    def start(g):
        merge(g)
        products(g)
        if g in A_GROUPS:
            rs_y(g)
        else:
            rs_1(g)

    def rs(g, s):
        rs_1(g) if s == 1 else rs_s(g, s)

    def ag(g, s):
        ag_1(g) if s == 1 else ag_end(g) if s == 5 else ag_s(g, s)

    def rows_done(k):
        for d in (k,) if k in (0, 4) else (k, -k):
            down(zat(d))

    tasks = {
        "start": start, "rs": rs, "pass": rs_pass, "hid": hidden, "ag": ag, "fin": ag_fin,
        "od": lambda: z_pass(1, od), "mdown": merge_down, "down": rows_done,
    }
    for name, *rest in ORDER:
        tasks[name](*rest)

    wait_recv(orec, out_sem.at[1])
    for p in range(4):
        total = obuf[core * 4 + p, chip].astype(F32)
        for k in range(15):
            total = total + orec[k, p].astype(F32)
        out_ref[p] = total.astype(BF)

    wait_send(orec, out_sem.at[0])
    wait_send(orec, gather_send.at[0])
    wait_send(ibuf.at[pl.ds(0, 15)], gather_send.at[1])
    wait_send(ogu.at[pl.ds(0, 15 * 112)], gather_send.at[2])
    wait_send(od.at[pl.ds(0, 15 * 112)], gather_send.at[3])
    for g in range(GROUPS):
        cols = pl.ds(g * GW, GW)
        if g in A_GROUPS:
            wait_send(part.at[g, pl.ds(0, 7), 0], ring_send.at[0, g])
            wait_send(part.at[g, :, 0], ring_send.at[1, g])
        else:
            wait_send(part.at[g, pl.ds(0, 7)], ring_send.at[0, g])
            wait_send(part.at[g, 0, 0], ring_send.at[1, g])
        if g in AGY:
            wait_send(hid.at[pl.ds(0, 7), 0, :, cols], ring_send.at[2, g])
            wait_send(hid.at[:, 0, :, cols], ring_send.at[3, g])
        else:
            wait_send(hid.at[pl.ds(0, 7), :, :, cols], ring_send.at[2, g])
            wait_send(hid.at[0, 0, :, cols], ring_send.at[3, g])


def layer(pick, order, tokens, *arrays):
    vmem = pl.BlockSpec(memory_space=pltpu.VMEM)
    hbm = pl.BlockSpec(memory_space=pl.ANY)
    smem = pl.BlockSpec(memory_space=pltpu.SMEM)
    dma = pltpu.SemaphoreType.DMA
    return pl.pallas_call(
        kernel,
        out_shape=jax.ShapeDtypeStruct((4, 16, 512), BF),
        in_specs=[smem, vmem, vmem] + [hbm] * 9,
        out_specs=vmem,
        scratch_shapes=[pltpu.VMEM(a.shape, BF) for a in arrays[:6]] + [
            pltpu.VMEM((512, 1792), BF),
            pltpu.VMEM((512, 1792), BF),
            pltpu.VMEM((1792, 512), BF),
            pltpu.VMEM((8, 128, 512), BF),
            pltpu.VMEM((16, 2, 32, 128), BF),
            pltpu.VMEM((1792, 128), BF),
            pltpu.VMEM((1792, 128), BF),
            pltpu.VMEM((3, 512, 128), BF),
            pltpu.VMEM((GROUPS, 8, 2, 64, 2 * GW), BF),
            pltpu.VMEM((NA, 8, 64, 2 * GW), BF),
            pltpu.VMEM((NA, 2, 4, 64, 2 * GW), BF),
            pltpu.VMEM((NB, 2, 4, 2, 64, 2 * GW), BF),
            pltpu.VMEM((NB, 64, 2 * GW), BF),
            pltpu.VMEM((8, 2, 64, GROUPS * GW), BF),
            pltpu.VMEM((8, 8, 16, 512), BF),
            pltpu.VMEM((15, 4, 16, 512), BF),
            dma((9,)),
            dma((2, 8)),
            dma((2, 8)),
            dma((2, 2, 8)),
            dma((4,)),
            dma((GROUPS, 2, 4)),
            dma((GROUPS, 8)),
            dma((GROUPS, 2, 4)),
            dma((GROUPS,)),
            dma((4, GROUPS)),
            dma((2,)),
        ],
        compiler_params=pltpu.CompilerParams(
            collective_id=0, has_side_effects=True, vmem_limit_bytes=56 * 2**20
        ),
    )(pick, order, tokens, *arrays)


def body(
    tokens, row_order, adapter_id, gate_weight, up_weight, down_weight,
    gate_inner, gate_outer, up_inner, up_outer, down_inner, down_outer,
):
    swap = lambda a: jnp.swapaxes(a, 1, 2)
    return layer(
        adapter_id, row_order.reshape(1, 64), tokens,
        gate_inner, up_inner, swap(down_inner), gate_outer, up_outer, swap(down_outer),
        gate_weight, up_weight, down_weight,
    ).reshape(64, 512)


def solution(mesh):
    return jax.shard_map(
        body,
        mesh=mesh,
        in_specs=(
            P("col", "row"),
            P("col"),
            P(),
            P("row", "col"),
            P("row", "col"),
            P("col", "row"),
            P(None, ("row", "col"), None),
            P(None, None, ("col", "row")),
            P(None, ("row", "col"), None),
            P(None, None, ("col", "row")),
            P(None, ("col", "row"), None),
            P(None, None, ("row", "col")),
        ),
        out_specs=P("col", "row"),
        check_vma=False,
    )
```

```python
import functools

import jax
import jax.numpy as jnp
from jax import lax
from jax.experimental import pallas as pl
from jax.experimental.pallas import tpu as pltpu
from jax.sharding import PartitionSpec as P

MESH = pl.DeviceIdType.MESH
BF = jnp.bfloat16
F32 = jnp.float32
GROUPS = 7
GW = 256
A_GROUPS = (1, 3, 5)
B_GROUPS = (0, 2, 4, 6)
NA, NB = len(A_GROUPS), len(B_GROUPS)
AGY = (0, 2, 4, 6)
AGZ = (1, 3, 5)
CW, CCW = 0, 1
ORDER = (
    ("start", 2), ("ipass",), ("tout",), ("start", 4), ("start", 5), ("start", 6), ("start", 0), ("rs", 2, 2),
    ("start", 3), ("rs", 5, 1), ("rs", 4, 2), ("rs", 6, 2), ("rs", 5, 2), ("rs", 2, 3), ("start", 1), ("rs", 0, 2),
    ("rs", 3, 1), ("rs", 6, 3), ("rs", 4, 3), ("rs", 5, 3), ("rs", 0, 3), ("rs", 1, 1), ("rs", 2, 4), ("rs", 4, 4),
    ("tmid",), ("gpass",), ("rs", 0, 4), ("od",), ("rs", 1, 2), ("pass", 2), ("rs", 5, 4), ("rs", 3, 2), ("pass", 4),
    ("gend",), ("rs", 6, 4), ("pass", 0), ("rs", 1, 3), ("mdown",), ("tend",), ("hid", 2), ("hid", 4), ("rs", 3, 3),
    ("hid", 0), ("pass", 6), ("hid", 5), ("rs", 1, 4), ("ag", 2, 2), ("ag", 4, 2), ("rs", 3, 4), ("ag", 0, 2),
    ("hid", 6), ("hid", 1), ("ag", 5, 1), ("ag", 2, 3), ("hid", 3), ("ag", 0, 3), ("ag", 6, 2), ("ag", 1, 1),
    ("ag", 5, 2), ("ag", 3, 1), ("ag", 6, 3), ("ag", 2, 4), ("ag", 4, 3), ("ag", 1, 2), ("down", 0), ("ag", 0, 4),
    ("ag", 3, 2), ("ag", 2, 5), ("ag", 6, 4), ("ag", 5, 3), ("ag", 4, 4), ("ag", 1, 3), ("ag", 3, 3), ("down", 1),
    ("ag", 5, 4), ("ag", 6, 5), ("down", 2), ("ag", 1, 4), ("ag", 0, 5), ("ag", 3, 4), ("ag", 4, 5), ("ag", 5, 5),
    ("down", 3), ("ag", 1, 5), ("ag", 3, 5), ("down", 4),
)
T00 = (((0,), (0,)), ((), ()))
T11 = (((1,), (1,)), ((), ()))


def dot(a, b, dims=(((1,), (0,)), ((), ()))):
    return lax.dot_general(a, b, dims, preferred_element_type=F32)


def kernel(
    pick_ref, order_ref, tokens_ref, gi_hbm, ui_hbm, di_hbm, go_hbm, uo_hbm, do_hbm, gate_hbm, up_hbm, down_hbm, out_ref,
    gi, ui, di, go, uo, do,
    wg, wu, wd, x, ibuf, ogu, od, im, tsend, trec, tall, tbig, part, yrec_a, zrec_a, zrec_b, yrec_b, hid, obuf, orec,
    load_sem, x_sem, i_sem, o_sem, t_sem, gather_send,
    rsz_recv, rsy_recv, agz_recv, agy_recv, ring_send, out_sem, out_recv,
):
    row, col = lax.axis_index("row"), lax.axis_index("col")
    yh, z = row // 8, row % 8
    chip, core = col // 2, col % 2
    zat = lambda k: (z + k + 8) % 8
    up_dev = (yh * 8 + zat(1), col)
    down_dev = (yh * 8 + zat(-1), col)
    y_dev = ((1 - yh) * 8 + z, col)
    sib_dev = (row, chip * 2 + 1 - core)
    ring_dev = (up_dev, down_dev)

    def remote(src, dst, send, recv, dev):
        return pltpu.make_async_remote_copy(src, dst, send, recv, device_id=dev, device_id_type=MESH)

    def wait_recv(dst, recv):
        remote(dst, dst, gather_send.at[0], recv, y_dev).wait_recv()

    def wait_send(src, send):
        remote(src, src, send, out_sem.at[1], y_dev).wait_send()

    pools = ((go_hbm, go), (uo_hbm, uo), (gi_hbm, gi), (ui_hbm, ui), (di_hbm, di), (do_hbm, do))
    weights = ((gate_hbm, wg), (up_hbm, wu), (down_hbm, wd))
    loads = [pltpu.make_async_copy(src, dst, load_sem.at[i]) for i, (src, dst) in enumerate(pools + weights)]
    for load in loads:
        load.start()

    barrier = pltpu.get_barrier_semaphore()
    for k in range(1, 16):
        pl.semaphore_signal(barrier, inc=1, device_id=(row, (col + k) % 16), device_id_type=MESH)
    for k in range(1, 16):
        pl.semaphore_signal(barrier, inc=1, device_id=((row + k) % 16, col), device_id_type=MESH)

    def g_at(r):
        return ogu.at[pl.ds(pl.multiple_of(r * 112, 16), 112)]

    def d_at(r):
        return od.at[r]

    def x_at(chip_, core_):
        return x.at[pl.ds(core_ * 4, 4), pl.ds(pl.multiple_of(chip_ * 16, 16), 16)]

    k = pick_ref[0]
    r128 = lax.broadcasted_iota(jnp.int32, (64, 128), 0)
    c128 = lax.broadcasted_iota(jnp.int32, (64, 128), 1)
    left = jnp.where(r128 == c128, 1.0, 0.0).astype(BF)
    right = jnp.where(r128 + 64 == c128, 1.0, 0.0).astype(BF)
    one_hot = jnp.where(lax.broadcasted_iota(jnp.int32, (64, 64), 0) == order_ref[...] % 64, 1.0, 0.0).astype(BF)
    x_at(chip, core)[...] = dot(one_hot, tokens_ref[...], T00).astype(BF).reshape(4, 16, 512)
    loads[0].wait()
    loads[1].wait()
    g_at(row)[...] = (dot(go[k], left, T00) + dot(uo[k], right, T00)).astype(BF)
    loads[2].wait()
    loads[3].wait()
    ibuf[col, 0] = (dot(gi[k], left) + dot(ui[k], right)).astype(BF)
    loads[4].wait()
    loads[5].wait()
    ibuf[col, 1] = (dot(do[k], left) + dot(do[k], right)).astype(BF)
    low, high = dot(di[k], left, T00), dot(di[k], right, T00)[64:112]
    od[row] = (low[0:64] + jnp.concatenate([high, jnp.zeros((16, 128), F32)], axis=0)).astype(BF)
    pl.semaphore_wait(barrier, 30)

    far = (4, 3, 5, 2, 6, 1, 7)
    near = (1, 7, 2, 6, 3, 5, 4)

    def z_send(n, at):
        here = at(row)
        for k in far:
            remote(here, here, gather_send.at[2 + n], o_sem.at[n, 0, k], (yh * 8 + zat(k), col)).start()
        remote(here, here, gather_send.at[2 + n], o_sem.at[n, 1, 0], y_dev).start()

    def col_send(here, n, sem):
        for k in near:
            remote(here, here, gather_send.at[n], sem.at[0, k], (row, (chip + k) % 8 * 2 + core)).start()
        remote(here, here, gather_send.at[n], sem.at[1, 0], sib_dev).start()

    def z_pass(n, at):
        for k in near:
            here = at(yh * 8 + zat(-k))
            wait_recv(here, o_sem.at[n, 0, k])
            remote(here, here, gather_send.at[2 + n], o_sem.at[n, 1, k], y_dev).start()

    def z_end(n, at):
        for k in range(8):
            wait_recv(at((1 - yh) * 8 + zat(-k)), o_sem.at[n, 1, k])

    def col_pass(at, n, sem):
        for k in near:
            here = at((chip + 8 - k) % 8, core)
            wait_recv(here, sem.at[0, k])
            remote(here, here, gather_send.at[n], sem.at[1, k], sib_dev).start()

    def col_end(at, n, sem):
        for k in range(8):
            wait_recv(at((chip + 8 - k) % 8, 1 - core), sem.at[1, k])

    i_at = lambda chip_, core_: ibuf.at[chip_ * 2 + core_]
    col_send(x_at(chip, core), 0, x_sem)
    z_send(0, g_at)
    col_send(i_at(chip, core), 1, i_sem)
    z_send(1, d_at)
    col_pass(x_at, 0, x_sem)
    loads[6].wait()
    loads[7].wait()
    col_end(x_at, 0, x_sem)

    t_role = (yh == col // 8) & (z // 4 == core)
    t_from = lambda j: yh * 8 + j * 2 + z // 4

    def t_out():
        col_end(i_at, 1, i_sem)
        lane = lax.broadcasted_iota(jnp.int32, (512, 128), 1)
        im[0] = ibuf[:, 0].reshape(512, 128)
        narrow = ibuf[:, 1].reshape(512, 128)
        im[1] = jnp.where(lane < 64, narrow, jnp.zeros_like(narrow))
        im[2] = jnp.where(lane >= 64, narrow, jnp.zeros_like(narrow))
        tsend[...] = dot(x_at(chip, core)[...].reshape(64, 512), im[0]).reshape(4, 16, 128)
        for p in range(4):
            to = col // 8 * 8 + core * 4 + p

            @pl.when(to != row)
            def _():
                remote(tsend.at[p], trec.at[(to + 15 - row) % 16], t_sem.at[0], t_sem.at[1], (to, col)).start()

    def t_mid():
        @pl.when(t_role)
        def _():
            wait_recv(trec, t_sem.at[1])
            total = tsend[z % 4]
            for k in range(15):
                total = total + trec[k]
            mine = tall.at[chip % 4]
            mine[...] = total.astype(BF)
            for k in range(1, 16):
                remote(mine, mine, t_sem.at[2], t_sem.at[3 + chip % 4], (row, (col + k) % 16)).start()

    def t_end():
        for j in range(4):
            @pl.when(t_from(j) != col)
            def _():
                wait_recv(tall.at[j], t_sem.at[3 + j])

    def merge_down():
        z_end(1, d_at)
        loads[8].wait()

        @pl.loop(0, 16)
        def _(r):
            for first, size, n in ((0, 64, 1), (64, 48, 2)):
                at = pl.ds(pl.multiple_of(r * 112 + first, 16), size)
                low = dot(od[r, 0:size], im[n], T11)
                wd[at] = (wd[at].astype(F32) + 2.0 * low).astype(BF)

    def products(g):
        cols = slice(g * GW, (g + 1) * GW)

        @pl.loop(0, 2)
        def _(i):
            rows = x[pl.ds(i * 4, 4)].reshape(512, 512)
            for half, w in enumerate((wg, wu)):
                term = dot(rows, w[:, cols])
                part[g, pl.ds(i * 4, 4), :, :, half * GW:(half + 1) * GW] = term.astype(BF).reshape(4, 2, 64, GW)

    def rs_refs(g):
        if g in A_GROUPS:
            n = A_GROUPS.index(g)
            return zrec_a.at[n], (lambda d: part.at[g, d, yh]), yrec_a.at[n]
        n = B_GROUPS.index(g)
        return zrec_b.at[n], (lambda d: part.at[g, d]), None

    def lanes(half):
        return pl.ds(half * GW, GW)

    def rs_y(g):
        _, _, yrec = rs_refs(g)
        for k in (4, 3, 5, 2, 6, 1, 7, 0):
            d = zat(k)
            remote(part.at[g, d, 1 - yh], yrec.at[d], ring_send.at[1, g], rsy_recv.at[g, k], y_dev).start()

    def y_wait(g, k):
        _, _, yrec = rs_refs(g)
        wait_recv(yrec.at[zat(k)], rsy_recv.at[g, k])

    def rs_1(g):
        zrec, at, yrec = rs_refs(g)
        d = zat(4)
        if yrec is not None:
            y_wait(g, 4)
            at(d)[...] = (at(d)[...].astype(F32) + yrec[d].astype(F32)).astype(BF)
        for way in (CW, CCW):
            remote(
                at(d).at[..., lanes(way)], zrec.at[way, 0].at[..., lanes(way)],
                ring_send.at[0, g], rsz_recv.at[g, way, 0], ring_dev[way],
            ).start()

    def rs_s(g, s):
        zrec, at, yrec = rs_refs(g)
        for way in (CW, CCW):
            d = zat(5 - s if way == CW else s - 5)
            if yrec is not None:
                y_wait(g, 5 - s if way == CW else s + 3)
            got = zrec.at[way, s - 2]
            spot = at(d)
            if s == 2:
                wait_recv(got.at[..., lanes(way)], rsz_recv.at[g, way, 0])
                for half in (0, 1):
                    total = spot[..., lanes(half)].astype(F32)
                    if yrec is not None:
                        total = total + yrec[d, :, lanes(half)].astype(F32)
                    if half == way:
                        total = total + got[..., lanes(half)].astype(F32)
                    if half == way or yrec is not None:
                        spot[..., lanes(half)] = total.astype(BF)
            else:
                wait_recv(got, rsz_recv.at[g, way, s - 2])
                total = spot[...].astype(F32) + got[...].astype(F32)
                if yrec is not None:
                    total = total + yrec[d].astype(F32)
                spot[...] = total.astype(BF)
            remote(spot, zrec.at[way, s - 1], ring_send.at[0, g], rsz_recv.at[g, way, s - 1], ring_dev[way]).start()

    def rs_end(g):
        zrec, at, _ = rs_refs(g)
        for way in (CW, CCW):
            wait_recv(zrec.at[way, 3], rsz_recv.at[g, way, 3])

    def rs_pass(g):
        rs_end(g)
        zrec, at, _ = rs_refs(g)
        away = part.at[g, z, 1 - yh]
        total = away[...].astype(F32) + zrec[CW, 3, 1 - yh].astype(F32) + zrec[CCW, 3, 1 - yh].astype(F32)
        away[...] = total.astype(BF)
        remote(away, yrec_b.at[B_GROUPS.index(g)], ring_send.at[1, g], rsy_recv.at[g, 0], y_dev).start()

    def hidden(g):
        if g in A_GROUPS:
            rs_end(g)
            y_wait(g, 0)
            zrec, at, yrec = rs_refs(g)
            terms = (part.at[g, z, yh], yrec.at[z], zrec.at[CW, 3], zrec.at[CCW, 3])
        else:
            n = B_GROUPS.index(g)
            wait_recv(yrec_b.at[n], rsy_recv.at[g, 0])
            terms = (part.at[g, z, yh], zrec_b.at[n, CW, 3, yh], zrec_b.at[n, CCW, 3, yh], yrec_b.at[n])
        sums = []
        pair = tall[...].reshape(64, 128)
        lane = lax.broadcasted_iota(jnp.int32, (64, 128), 1)
        for half in (0, 1):
            total = terms[0][:, lanes(half)].astype(F32)
            for term in terms[1:]:
                total = total + term[:, lanes(half)].astype(F32)
            one = jnp.where((lane < 64) if half == 0 else (lane >= 64), pair, jnp.zeros_like(pair))
            sums.append(total + 2.0 * dot(one, ogu[g * GW:(g + 1) * GW], T11))
        gate, up = sums
        hid[z, yh, :, g * GW:(g + 1) * GW] = (gate / (1.0 + jnp.exp(-gate)) * up).astype(BF)
        ag_y(g, 0)
        if g in AGY:
            ag_z(g)

    def h_at(g, d, s=1, way=None):
        lo, n = (g * GW, GW) if s < 4 else (g * GW + way * GW // 2, GW // 2)
        if g in AGY:
            return hid.at[d, yh, :, pl.ds(lo, n)]
        return hid.at[d, :, :, pl.ds(lo, n)]

    def ag_y(g, k):
        ref = hid.at[zat(k), yh, :, pl.ds(g * GW, GW)]
        remote(ref, ref, ring_send.at[3, g], agy_recv.at[g, k % 8], y_dev).start()

    def ag_z(g):
        for way in (CW, CCW):
            ref = h_at(g, z)
            remote(ref, ref, ring_send.at[2, g], agz_recv.at[g, way, 0], ring_dev[way]).start()

    def ag_y_wait(g, k):
        wait_recv(hid.at[zat(k), 1 - yh, :, pl.ds(g * GW, GW)], agy_recv.at[g, k % 8])

    def ag_1(g):
        ag_y_wait(g, 0)
        ag_z(g)

    def ag_s(g, s):
        for way in (CW, CCW):
            d = zat(1 - s if way == CW else s - 1)
            wait_recv(h_at(g, d), agz_recv.at[g, way, s - 2])
            ref = h_at(g, d, s, way)
            remote(ref, ref, ring_send.at[2, g], agz_recv.at[g, way, s - 1], ring_dev[way]).start()
            if g in AGY:
                ag_y(g, 1 - s if way == CW else s - 1)

    def ag_end(g):
        for way in (CW, CCW):
            wait_recv(h_at(g, zat(4), 4, way), agz_recv.at[g, way, 3])
        if g in AGY:
            ag_y(g, 4)

    def down(*offsets):
        places = [zat(k) for k in offsets]
        n = len(places)
        for g in AGY:
            for k in offsets:
                ag_y_wait(g, k)
        rows = [hid[d].reshape(128, GROUPS * GW) for d in places]
        term = dot(rows[0] if n == 1 else jnp.concatenate(rows, axis=0), wd[...])
        for m, d in enumerate(places):
            obuf[d] = term[m * 128:(m + 1) * 128].astype(BF).reshape(8, 16, 512)
        for d in places:
            @pl.loop(0, 8)
            def _(j):
                to = j * 2 + d // 4

                @pl.when(to != col)
                def _():
                    remote(
                        obuf.at[d, j], orec.at[(to + 15 - col) % 16, d % 4],
                        out_sem.at[0], out_recv.at[d % 4], (row, to),
                    ).start()

    def start(g):
        products(g)
        if g in A_GROUPS:
            rs_y(g)
        else:
            rs_1(g)

    def rs(g, s):
        rs_1(g) if s == 1 else rs_s(g, s)

    def ag(g, s):
        ag_1(g) if s == 1 else ag_end(g) if s == 5 else ag_s(g, s)

    def rows_done(k):
        down(*((k,) if k in (0, 4) else (k, -k)))

    tasks = {
        "start": start, "rs": rs, "pass": rs_pass, "hid": hidden, "ag": ag,
        "ipass": lambda: col_pass(i_at, 1, i_sem), "gpass": lambda: z_pass(0, g_at), "gend": lambda: z_end(0, g_at),
        "tout": t_out, "tmid": t_mid, "tend": t_end,
        "od": lambda: z_pass(1, d_at), "mdown": merge_down, "down": rows_done,
    }
    for name, *rest in ORDER:
        tasks[name](*rest)

    for k in (0, 1, 7, 2, 6, 3, 5, 4):
        d = zat(k)
        p = d % 4

        @pl.when(d // 4 == core)
        def _():
            wait_recv(orec.at[:, p], out_recv.at[p])
            total = obuf[d, chip].astype(F32)
            for n in range(15):
                total = total + orec[n, p].astype(F32)
            out_ref[p] = total.astype(BF)

    wait_send(orec, out_sem.at[0])
    wait_send(orec, gather_send.at[0])
    wait_send(ibuf.at[pl.ds(0, 15)], gather_send.at[1])
    wait_send(ogu.at[pl.ds(0, 15 * 112)], gather_send.at[2])
    wait_send(od.at[pl.ds(0, 15)], gather_send.at[3])
    sent = col // 8 * 8 + core * 4

    @pl.when((row >= sent) & (row < sent + 4))
    def _():
        wait_send(tsend.at[pl.ds(0, 3)], t_sem.at[0])

    @pl.when((row < sent) | (row >= sent + 4))
    def _():
        wait_send(tsend, t_sem.at[0])

    @pl.when(t_role)
    def _():
        wait_send(tbig, t_sem.at[2])

    for g in range(GROUPS):
        cols = pl.ds(g * GW, GW)
        if g in A_GROUPS:
            wait_send(part.at[g, pl.ds(0, 7), 0], ring_send.at[0, g])
            wait_send(part.at[g, :, 0], ring_send.at[1, g])
        else:
            wait_send(part.at[g, pl.ds(0, 7)], ring_send.at[0, g])
            wait_send(part.at[g, 0, 0], ring_send.at[1, g])
        if g in AGY:
            wait_send(hid.at[pl.ds(0, 7), 0, :, cols], ring_send.at[2, g])
            wait_send(hid.at[:, 0, :, cols], ring_send.at[3, g])
        else:
            wait_send(hid.at[pl.ds(0, 7), :, :, cols], ring_send.at[2, g])
            wait_send(hid.at[0, 0, :, cols], ring_send.at[3, g])


def layer(pick, order, tokens, *arrays):
    vmem = pl.BlockSpec(memory_space=pltpu.VMEM)
    hbm = pl.BlockSpec(memory_space=pl.ANY)
    smem = pl.BlockSpec(memory_space=pltpu.SMEM)
    dma = pltpu.SemaphoreType.DMA
    return pl.pallas_call(
        kernel,
        out_shape=jax.ShapeDtypeStruct((4, 16, 512), BF),
        in_specs=[smem, vmem, vmem] + [hbm] * 9,
        out_specs=vmem,
        scratch_shapes=[pltpu.VMEM(a.shape, BF) for a in arrays[:6]] + [
            pltpu.VMEM((512, 1792), BF),
            pltpu.VMEM((512, 1792), BF),
            pltpu.VMEM((1792, 512), BF),
            pltpu.VMEM((8, 128, 512), BF),
            pltpu.VMEM((16, 2, 32, 128), BF),
            pltpu.VMEM((1792, 128), BF),
            pltpu.VMEM((16, 64, 128), BF),
            pltpu.VMEM((3, 512, 128), BF),
            pltpu.VMEM((4, 16, 128), F32),
            pltpu.VMEM((15, 16, 128), F32),
            pltpu.VMEM((4, 16, 128), BF),
            pltpu.VMEM((15, 16, 128), BF),
            pltpu.VMEM((GROUPS, 8, 2, 64, 2 * GW), BF),
            pltpu.VMEM((NA, 8, 64, 2 * GW), BF),
            pltpu.VMEM((NA, 2, 4, 64, 2 * GW), BF),
            pltpu.VMEM((NB, 2, 4, 2, 64, 2 * GW), BF),
            pltpu.VMEM((NB, 64, 2 * GW), BF),
            pltpu.VMEM((8, 2, 64, GROUPS * GW), BF),
            pltpu.VMEM((8, 8, 16, 512), BF),
            pltpu.VMEM((15, 4, 16, 512), BF),
            dma((9,)),
            dma((2, 8)),
            dma((2, 8)),
            dma((2, 2, 8)),
            dma((7,)),
            dma((4,)),
            dma((GROUPS, 2, 4)),
            dma((GROUPS, 8)),
            dma((GROUPS, 2, 4)),
            dma((GROUPS, 8)),
            dma((4, GROUPS)),
            dma((2,)),
            dma((4,)),
        ],
        compiler_params=pltpu.CompilerParams(
            collective_id=0, has_side_effects=True, vmem_limit_bytes=56 * 2**20
        ),
    )(pick, order, tokens, *arrays)


def body(
    tokens, row_order, adapter_id, gate_weight, up_weight, down_weight,
    gate_inner, gate_outer, up_inner, up_outer, down_inner, down_outer,
):
    swap = lambda a: jnp.swapaxes(a, 1, 2)
    return layer(
        adapter_id, row_order.reshape(1, 64), tokens,
        gate_inner, up_inner, swap(down_inner), gate_outer, up_outer, swap(down_outer),
        gate_weight, up_weight, down_weight,
    ).reshape(64, 512)


def solution(mesh):
    return jax.shard_map(
        body,
        mesh=mesh,
        in_specs=(
            P("col", "row"),
            P("col"),
            P(),
            P("row", "col"),
            P("row", "col"),
            P("col", "row"),
            P(None, ("row", "col"), None),
            P(None, None, ("col", "row")),
            P(None, ("row", "col"), None),
            P(None, None, ("col", "row")),
            P(None, ("col", "row"), None),
            P(None, None, ("row", "col")),
        ),
        out_specs=P("col", "row"),
        check_vma=False,
    )
```

```python
import functools

import jax
import jax.numpy as jnp
from jax import lax
from jax.experimental import pallas as pl
from jax.experimental.pallas import tpu as pltpu
from jax.sharding import PartitionSpec as P

MESH = pl.DeviceIdType.MESH
BF = jnp.bfloat16
F32 = jnp.float32
GROUPS = 7
GW = 256
A_GROUPS = (1, 3, 5)
B_GROUPS = (0, 2, 4, 6)
NA, NB = len(A_GROUPS), len(B_GROUPS)
AGY = (0, 2, 4)
AGZ = (1, 3, 5, 6)
CW, CCW = 0, 1
ORDER = (
    ("start", 0), ("start", 2), ("start", 6), ("start", 5), ("start", 4), ("rs", 0, 2), ("start", 3), ("ipass",),
    ("rs", 2, 2), ("rs", 4, 2), ("rs", 6, 2), ("rs", 5, 1), ("rs", 0, 3), ("rs", 2, 3), ("tout",), ("rs", 3, 1),
    ("rs", 6, 3), ("rs", 5, 2), ("start", 1), ("rs", 0, 4), ("rs", 3, 2), ("rs", 2, 4), ("rs", 1, 1), ("rs", 5, 3),
    ("rs", 4, 3), ("rs", 6, 4), ("gpass",), ("pass", 2), ("rs", 1, 2), ("pass", 0), ("tmid",), ("od",), ("rs", 3, 3),
    ("rs", 5, 4), ("rs", 4, 4), ("gend",), ("pass", 6), ("tend",), ("rs", 1, 3), ("hid", 0), ("rs", 3, 4), ("hid", 2),
    ("hid", 5), ("hid", 6), ("pass", 4), ("ag", 0, 2), ("rs", 1, 4), ("ag", 2, 2), ("hid", 3), ("ag", 5, 1),
    ("ag", 6, 1), ("mdown",), ("hid", 4), ("ag", 0, 3), ("hid", 1), ("ag", 2, 3), ("ag", 3, 1), ("ag", 5, 2),
    ("ag", 4, 2), ("ag", 6, 2), ("ag", 1, 1), ("ag", 2, 4), ("ag", 3, 2), ("ag", 4, 3), ("ag", 5, 3), ("down", 0),
    ("ag", 1, 2), ("ag", 6, 3), ("ag", 0, 4), ("down", 1), ("ag", 3, 3), ("ag", 4, 4), ("ag", 1, 3), ("ag", 2, 5),
    ("down", 2), ("ag", 5, 4), ("ag", 6, 4), ("ag", 0, 5), ("ag", 3, 4), ("ag", 4, 5), ("ag", 1, 4), ("down", 3),
    ("ag", 3, 5), ("ag", 6, 5), ("ag", 5, 5), ("ag", 1, 5), ("down", 4),
)
T00 = (((0,), (0,)), ((), ()))
T11 = (((1,), (1,)), ((), ()))


def dot(a, b, dims=(((1,), (0,)), ((), ()))):
    return lax.dot_general(a, b, dims, preferred_element_type=F32)


def kernel(
    pick_ref, order_ref, tokens_ref, gi_hbm, ui_hbm, di_hbm, go_hbm, uo_hbm, do_hbm, gate_hbm, up_hbm, down_hbm, out_ref,
    gi, ui, di, go, uo, do,
    wg, wu, wd, x, ibuf, ogu, od, im, tsend, trec, tall, tbig, part, yrec_a, zrec_a, zrec_b, yrec_b, hid, obuf, orec,
    load_sem, x_sem, i_sem, o_sem, t_sem, gather_send,
    rsz_recv, rsy_recv, agz_recv, agy_recv, ring_send, out_sem, out_recv,
):
    row, col = lax.axis_index("row"), lax.axis_index("col")
    yh, z = row // 8, row % 8
    chip, core = col // 2, col % 2
    zat = lambda k: (z + k + 8) % 8
    up_dev = (yh * 8 + zat(1), col)
    down_dev = (yh * 8 + zat(-1), col)
    y_dev = ((1 - yh) * 8 + z, col)
    sib_dev = (row, chip * 2 + 1 - core)
    ring_dev = (up_dev, down_dev)

    def remote(src, dst, send, recv, dev):
        return pltpu.make_async_remote_copy(src, dst, send, recv, device_id=dev, device_id_type=MESH)

    def wait_recv(dst, recv):
        remote(dst, dst, gather_send.at[0], recv, y_dev).wait_recv()

    def wait_send(src, send):
        remote(src, src, send, out_sem.at[1], y_dev).wait_send()

    pools = ((go_hbm, go), (uo_hbm, uo), (gi_hbm, gi), (ui_hbm, ui), (di_hbm, di), (do_hbm, do))
    weights = ((gate_hbm, wg), (up_hbm, wu), (down_hbm, wd))
    loads = [pltpu.make_async_copy(src, dst, load_sem.at[i]) for i, (src, dst) in enumerate(pools + weights)]
    for load in loads:
        load.start()

    barrier = pltpu.get_barrier_semaphore()
    for k in range(1, 16):
        pl.semaphore_signal(barrier, inc=1, device_id=(row, (col + k) % 16), device_id_type=MESH)
    for k in range(1, 16):
        pl.semaphore_signal(barrier, inc=1, device_id=((row + k) % 16, col), device_id_type=MESH)

    def g_at(r):
        return ogu.at[pl.ds(pl.multiple_of(r * 112, 16), 112)]

    def d_at(r):
        return od.at[r]

    def x_at(chip_, core_):
        return x.at[pl.ds(core_ * 4, 4), pl.ds(pl.multiple_of(chip_ * 16, 16), 16)]

    k = pick_ref[0]
    r128 = lax.broadcasted_iota(jnp.int32, (64, 128), 0)
    c128 = lax.broadcasted_iota(jnp.int32, (64, 128), 1)
    left = jnp.where(r128 == c128, 1.0, 0.0).astype(BF)
    right = jnp.where(r128 + 64 == c128, 1.0, 0.0).astype(BF)
    one_hot = jnp.where(lax.broadcasted_iota(jnp.int32, (64, 64), 0) == order_ref[...] % 64, 1.0, 0.0).astype(BF)
    x_at(chip, core)[...] = dot(one_hot, tokens_ref[...], T00).astype(BF).reshape(4, 16, 512)
    loads[0].wait()
    loads[1].wait()
    g_at(row)[...] = (dot(go[k], left, T00) + dot(uo[k], right, T00)).astype(BF)
    loads[2].wait()
    loads[3].wait()
    ibuf[col, 0] = (dot(gi[k], left) + dot(ui[k], right)).astype(BF)
    loads[4].wait()
    loads[5].wait()
    ibuf[col, 1] = (dot(do[k], left) + dot(do[k], right)).astype(BF)
    low, high = dot(di[k], left, T00), dot(di[k], right, T00)[64:112]
    od[row] = (low[0:64] + jnp.concatenate([high, jnp.zeros((16, 128), F32)], axis=0)).astype(BF)
    pl.semaphore_wait(barrier, 30)

    far = (4, 3, 5, 2, 6, 1, 7)
    near = (1, 7, 2, 6, 3, 5, 4)

    def z_send(n, at):
        here = at(row)
        for k in far:
            remote(here, here, gather_send.at[2 + n], o_sem.at[n, 0, k], (yh * 8 + zat(k), col)).start()
        remote(here, here, gather_send.at[2 + n], o_sem.at[n, 1, 0], y_dev).start()

    def col_send(here, n, sem):
        for k in near:
            remote(here, here, gather_send.at[n], sem.at[0, k], (row, (chip + k) % 8 * 2 + core)).start()
        remote(here, here, gather_send.at[n], sem.at[1, 0], sib_dev).start()

    def z_pass(n, at):
        for k in near:
            here = at(yh * 8 + zat(-k))
            wait_recv(here, o_sem.at[n, 0, k])
            remote(here, here, gather_send.at[2 + n], o_sem.at[n, 1, k], y_dev).start()

    def z_end(n, at):
        for k in range(8):
            wait_recv(at((1 - yh) * 8 + zat(-k)), o_sem.at[n, 1, k])

    def col_pass(at, n, sem):
        for k in near:
            here = at((chip + 8 - k) % 8, core)
            wait_recv(here, sem.at[0, k])
            remote(here, here, gather_send.at[n], sem.at[1, k], sib_dev).start()

    def col_end(at, n, sem):
        for k in range(8):
            wait_recv(at((chip + 8 - k) % 8, 1 - core), sem.at[1, k])

    i_at = lambda chip_, core_: ibuf.at[chip_ * 2 + core_]
    col_send(x_at(chip, core), 0, x_sem)
    z_send(0, g_at)
    col_send(i_at(chip, core), 1, i_sem)
    z_send(1, d_at)
    col_pass(x_at, 0, x_sem)
    loads[6].wait()
    loads[7].wait()
    col_end(x_at, 0, x_sem)

    t_role = (yh == col // 8) & (z // 4 == core)
    t_from = lambda j: yh * 8 + j * 2 + z // 4

    def t_out():
        col_end(i_at, 1, i_sem)
        lane = lax.broadcasted_iota(jnp.int32, (512, 128), 1)
        im[0] = ibuf[:, 0].reshape(512, 128)
        narrow = ibuf[:, 1].reshape(512, 128)
        im[1] = jnp.where(lane < 64, narrow, jnp.zeros_like(narrow))
        im[2] = jnp.where(lane >= 64, narrow, jnp.zeros_like(narrow))
        tsend[...] = dot(x_at(chip, core)[...].reshape(64, 512), im[0]).reshape(4, 16, 128)
        for p in range(4):
            to = col // 8 * 8 + core * 4 + p

            @pl.when(to != row)
            def _():
                remote(tsend.at[p], trec.at[(to + 15 - row) % 16], t_sem.at[0], t_sem.at[1], (to, col)).start()

    def t_mid():
        @pl.when(t_role)
        def _():
            wait_recv(trec, t_sem.at[1])
            total = tsend[z % 4]
            for k in range(15):
                total = total + trec[k]
            mine = tall.at[chip % 4]
            mine[...] = total.astype(BF)
            for k in range(1, 16):
                remote(mine, mine, t_sem.at[2], t_sem.at[3 + chip % 4], (row, (col + k) % 16)).start()

    def t_end():
        for j in range(4):
            @pl.when(t_from(j) != col)
            def _():
                wait_recv(tall.at[j], t_sem.at[3 + j])

    def merge_down():
        z_end(1, d_at)
        loads[8].wait()

        @pl.loop(0, 16)
        def _(r):
            for first, size, n in ((0, 64, 1), (64, 48, 2)):
                at = pl.ds(pl.multiple_of(r * 112 + first, 16), size)
                low = dot(od[r, 0:size], im[n], T11)
                wd[at] = (wd[at].astype(F32) + 2.0 * low).astype(BF)

    def products(g):
        cols = slice(g * GW, (g + 1) * GW)

        @pl.loop(0, 2)
        def _(i):
            rows = x[pl.ds(i * 4, 4)].reshape(512, 512)
            for half, w in enumerate((wg, wu)):
                term = dot(rows, w[:, cols])
                part[g, pl.ds(i * 4, 4), :, :, half * GW:(half + 1) * GW] = term.astype(BF).reshape(4, 2, 64, GW)

    def rs_refs(g):
        if g in A_GROUPS:
            n = A_GROUPS.index(g)
            return zrec_a.at[n], (lambda d: part.at[g, d, yh]), yrec_a.at[n]
        n = B_GROUPS.index(g)
        return zrec_b.at[n], (lambda d: part.at[g, d]), None

    def lanes(half):
        return pl.ds(half * GW, GW)

    def rs_y(g):
        _, _, yrec = rs_refs(g)
        for k in (4, 3, 5, 2, 6, 1, 7, 0):
            d = zat(k)
            remote(part.at[g, d, 1 - yh], yrec.at[d], ring_send.at[1, g], rsy_recv.at[g, k], y_dev).start()

    def y_wait(g, k):
        _, _, yrec = rs_refs(g)
        wait_recv(yrec.at[zat(k)], rsy_recv.at[g, k])

    def rs_1(g):
        zrec, at, yrec = rs_refs(g)
        d = zat(4)
        if yrec is not None:
            y_wait(g, 4)
            at(d)[...] = (at(d)[...].astype(F32) + yrec[d].astype(F32)).astype(BF)
        for way in (CW, CCW):
            remote(
                at(d).at[..., lanes(way)], zrec.at[way, 0].at[..., lanes(way)],
                ring_send.at[0, g], rsz_recv.at[g, way, 0], ring_dev[way],
            ).start()

    def rs_s(g, s):
        zrec, at, yrec = rs_refs(g)
        for way in (CW, CCW):
            d = zat(5 - s if way == CW else s - 5)
            if yrec is not None:
                y_wait(g, 5 - s if way == CW else s + 3)
            got = zrec.at[way, s - 2]
            spot = at(d)
            if s == 2:
                wait_recv(got.at[..., lanes(way)], rsz_recv.at[g, way, 0])
                for half in (0, 1):
                    total = spot[..., lanes(half)].astype(F32)
                    if yrec is not None:
                        total = total + yrec[d, :, lanes(half)].astype(F32)
                    if half == way:
                        total = total + got[..., lanes(half)].astype(F32)
                    if half == way or yrec is not None:
                        spot[..., lanes(half)] = total.astype(BF)
            else:
                wait_recv(got, rsz_recv.at[g, way, s - 2])
                total = spot[...].astype(F32) + got[...].astype(F32)
                if yrec is not None:
                    total = total + yrec[d].astype(F32)
                spot[...] = total.astype(BF)
            remote(spot, zrec.at[way, s - 1], ring_send.at[0, g], rsz_recv.at[g, way, s - 1], ring_dev[way]).start()

    def rs_end(g):
        zrec, at, _ = rs_refs(g)
        for way in (CW, CCW):
            wait_recv(zrec.at[way, 3], rsz_recv.at[g, way, 3])

    def rs_pass(g):
        rs_end(g)
        zrec, at, _ = rs_refs(g)
        away = part.at[g, z, 1 - yh]
        total = away[...].astype(F32) + zrec[CW, 3, 1 - yh].astype(F32) + zrec[CCW, 3, 1 - yh].astype(F32)
        away[...] = total.astype(BF)
        remote(away, yrec_b.at[B_GROUPS.index(g)], ring_send.at[1, g], rsy_recv.at[g, 0], y_dev).start()

    def hidden(g):
        if g in A_GROUPS:
            rs_end(g)
            y_wait(g, 0)
            zrec, at, yrec = rs_refs(g)
            terms = (part.at[g, z, yh], yrec.at[z], zrec.at[CW, 3], zrec.at[CCW, 3])
        else:
            n = B_GROUPS.index(g)
            wait_recv(yrec_b.at[n], rsy_recv.at[g, 0])
            terms = (part.at[g, z, yh], zrec_b.at[n, CW, 3, yh], zrec_b.at[n, CCW, 3, yh], yrec_b.at[n])
        sums = []
        pair = tall[...].reshape(64, 128)
        lane = lax.broadcasted_iota(jnp.int32, (64, 128), 1)
        for half in (0, 1):
            total = terms[0][:, lanes(half)].astype(F32)
            for term in terms[1:]:
                total = total + term[:, lanes(half)].astype(F32)
            one = jnp.where((lane < 64) if half == 0 else (lane >= 64), pair, jnp.zeros_like(pair))
            sums.append(total + 2.0 * dot(one, ogu[g * GW:(g + 1) * GW], T11))
        gate, up = sums
        hid[z, yh, :, g * GW:(g + 1) * GW] = (gate / (1.0 + jnp.exp(-gate)) * up).astype(BF)
        ag_y(g, 0)
        if g in AGY:
            ag_z(g)

    def h_at(g, d, s=1, way=None):
        lo, n = (g * GW, GW) if s < 4 else (g * GW + way * GW // 2, GW // 2)
        if g in AGY:
            return hid.at[d, yh, :, pl.ds(lo, n)]
        return hid.at[d, :, :, pl.ds(lo, n)]

    def ag_y(g, k):
        ref = hid.at[zat(k), yh, :, pl.ds(g * GW, GW)]
        remote(ref, ref, ring_send.at[3, g], agy_recv.at[g, k % 8], y_dev).start()

    def ag_z(g):
        for way in (CW, CCW):
            ref = h_at(g, z)
            remote(ref, ref, ring_send.at[2, g], agz_recv.at[g, way, 0], ring_dev[way]).start()

    def ag_y_wait(g, k):
        wait_recv(hid.at[zat(k), 1 - yh, :, pl.ds(g * GW, GW)], agy_recv.at[g, k % 8])

    def ag_1(g):
        ag_y_wait(g, 0)
        ag_z(g)

    def ag_s(g, s):
        for way in (CW, CCW):
            d = zat(1 - s if way == CW else s - 1)
            wait_recv(h_at(g, d), agz_recv.at[g, way, s - 2])
            ref = h_at(g, d, s, way)
            remote(ref, ref, ring_send.at[2, g], agz_recv.at[g, way, s - 1], ring_dev[way]).start()
            if g in AGY:
                ag_y(g, 1 - s if way == CW else s - 1)

    def ag_end(g):
        for way in (CW, CCW):
            wait_recv(h_at(g, zat(4), 4, way), agz_recv.at[g, way, 3])
        if g in AGY:
            ag_y(g, 4)

    def down(*offsets):
        places = [zat(k) for k in offsets]
        n = len(places)
        for g in AGY:
            for k in offsets:
                ag_y_wait(g, k)
        rows = [hid[d].reshape(128, GROUPS * GW) for d in places]
        term = dot(rows[0] if n == 1 else jnp.concatenate(rows, axis=0), wd[...])
        for m, d in enumerate(places):
            obuf[d] = term[m * 128:(m + 1) * 128].astype(BF).reshape(8, 16, 512)
        for d in places:
            @pl.loop(0, 8)
            def _(j):
                to = j * 2 + d // 4

                @pl.when(to != col)
                def _():
                    remote(
                        obuf.at[d, j], orec.at[(to + 15 - col) % 16, d % 4],
                        out_sem.at[0], out_recv.at[d % 4], (row, to),
                    ).start()

    def start(g):
        products(g)
        if g in A_GROUPS:
            rs_y(g)
        else:
            rs_1(g)

    def rs(g, s):
        rs_1(g) if s == 1 else rs_s(g, s)

    def ag(g, s):
        ag_1(g) if s == 1 else ag_end(g) if s == 5 else ag_s(g, s)

    def rows_done(k):
        down(*((k,) if k in (0, 4) else (k, -k)))

    tasks = {
        "start": start, "rs": rs, "pass": rs_pass, "hid": hidden, "ag": ag,
        "ipass": lambda: col_pass(i_at, 1, i_sem), "gpass": lambda: z_pass(0, g_at), "gend": lambda: z_end(0, g_at),
        "tout": t_out, "tmid": t_mid, "tend": t_end,
        "od": lambda: z_pass(1, d_at), "mdown": merge_down, "down": rows_done,
    }
    for name, *rest in ORDER:
        tasks[name](*rest)

    for k in (0, 1, 7, 2, 6, 3, 5, 4):
        d = zat(k)
        p = d % 4

        @pl.when(d // 4 == core)
        def _():
            wait_recv(orec.at[:, p], out_recv.at[p])
            total = obuf[d, chip].astype(F32)
            for n in range(15):
                total = total + orec[n, p].astype(F32)
            out_ref[p] = total.astype(BF)

    wait_send(orec, out_sem.at[0])
    wait_send(orec, gather_send.at[0])
    wait_send(ibuf.at[pl.ds(0, 15)], gather_send.at[1])
    wait_send(ogu.at[pl.ds(0, 15 * 112)], gather_send.at[2])
    wait_send(od.at[pl.ds(0, 15)], gather_send.at[3])
    sent = col // 8 * 8 + core * 4

    @pl.when((row >= sent) & (row < sent + 4))
    def _():
        wait_send(tsend.at[pl.ds(0, 3)], t_sem.at[0])

    @pl.when((row < sent) | (row >= sent + 4))
    def _():
        wait_send(tsend, t_sem.at[0])

    @pl.when(t_role)
    def _():
        wait_send(tbig, t_sem.at[2])

    for g in range(GROUPS):
        cols = pl.ds(g * GW, GW)
        if g in A_GROUPS:
            wait_send(part.at[g, pl.ds(0, 7), 0], ring_send.at[0, g])
            wait_send(part.at[g, :, 0], ring_send.at[1, g])
        else:
            wait_send(part.at[g, pl.ds(0, 7)], ring_send.at[0, g])
            wait_send(part.at[g, 0, 0], ring_send.at[1, g])
        if g in AGY:
            wait_send(hid.at[pl.ds(0, 7), 0, :, cols], ring_send.at[2, g])
            wait_send(hid.at[:, 0, :, cols], ring_send.at[3, g])
        else:
            wait_send(hid.at[pl.ds(0, 7), :, :, cols], ring_send.at[2, g])
            wait_send(hid.at[0, 0, :, cols], ring_send.at[3, g])


def layer(pick, order, tokens, *arrays):
    vmem = pl.BlockSpec(memory_space=pltpu.VMEM)
    hbm = pl.BlockSpec(memory_space=pl.ANY)
    smem = pl.BlockSpec(memory_space=pltpu.SMEM)
    dma = pltpu.SemaphoreType.DMA
    return pl.pallas_call(
        kernel,
        out_shape=jax.ShapeDtypeStruct((4, 16, 512), BF),
        in_specs=[smem, vmem, vmem] + [hbm] * 9,
        out_specs=vmem,
        scratch_shapes=[pltpu.VMEM(a.shape, BF) for a in arrays[:6]] + [
            pltpu.VMEM((512, 1792), BF),
            pltpu.VMEM((512, 1792), BF),
            pltpu.VMEM((1792, 512), BF),
            pltpu.VMEM((8, 128, 512), BF),
            pltpu.VMEM((16, 2, 32, 128), BF),
            pltpu.VMEM((1792, 128), BF),
            pltpu.VMEM((16, 64, 128), BF),
            pltpu.VMEM((3, 512, 128), BF),
            pltpu.VMEM((4, 16, 128), F32),
            pltpu.VMEM((15, 16, 128), F32),
            pltpu.VMEM((4, 16, 128), BF),
            pltpu.VMEM((15, 16, 128), BF),
            pltpu.VMEM((GROUPS, 8, 2, 64, 2 * GW), BF),
            pltpu.VMEM((NA, 8, 64, 2 * GW), BF),
            pltpu.VMEM((NA, 2, 4, 64, 2 * GW), BF),
            pltpu.VMEM((NB, 2, 4, 2, 64, 2 * GW), BF),
            pltpu.VMEM((NB, 64, 2 * GW), BF),
            pltpu.VMEM((8, 2, 64, GROUPS * GW), BF),
            pltpu.VMEM((8, 8, 16, 512), BF),
            pltpu.VMEM((15, 4, 16, 512), BF),
            dma((9,)),
            dma((2, 8)),
            dma((2, 8)),
            dma((2, 2, 8)),
            dma((7,)),
            dma((4,)),
            dma((GROUPS, 2, 4)),
            dma((GROUPS, 8)),
            dma((GROUPS, 2, 4)),
            dma((GROUPS, 8)),
            dma((4, GROUPS)),
            dma((2,)),
            dma((4,)),
        ],
        compiler_params=pltpu.CompilerParams(
            collective_id=0, has_side_effects=True, vmem_limit_bytes=56 * 2**20
        ),
    )(pick, order, tokens, *arrays)


def body(
    tokens, row_order, adapter_id, gate_weight, up_weight, down_weight,
    gate_inner, gate_outer, up_inner, up_outer, down_inner, down_outer,
):
    swap = lambda a: jnp.swapaxes(a, 1, 2)
    return layer(
        adapter_id, row_order.reshape(1, 64), tokens,
        gate_inner, up_inner, swap(down_inner), gate_outer, up_outer, swap(down_outer),
        gate_weight, up_weight, down_weight,
    ).reshape(64, 512)


def solution(mesh):
    return jax.shard_map(
        body,
        mesh=mesh,
        in_specs=(
            P("col", "row"),
            P("col"),
            P(),
            P("row", "col"),
            P("row", "col"),
            P("col", "row"),
            P(None, ("row", "col"), None),
            P(None, None, ("col", "row")),
            P(None, ("row", "col"), None),
            P(None, None, ("col", "row")),
            P(None, ("col", "row"), None),
            P(None, None, ("row", "col")),
        ),
        out_specs=P("col", "row"),
        check_vma=False,
    )
```

```python
import functools

import jax
import jax.numpy as jnp
from jax import lax
from jax.experimental import pallas as pl
from jax.experimental.pallas import tpu as pltpu
from jax.sharding import PartitionSpec as P

MESH = pl.DeviceIdType.MESH
BF = jnp.bfloat16
F32 = jnp.float32
GROUPS = 7
GW = 256
A_GROUPS = (1, 3, 5)
B_GROUPS = (0, 2, 4, 6)
NA, NB = len(A_GROUPS), len(B_GROUPS)
AGY = (0, 2, 4)
AGZ = (1, 3, 5, 6)
CW, CCW = 0, 1
ORDER = (
    ("start", 0), ("ipass",), ("gpass",), ("start", 4), ("start", 6), ("start", 2), ("start", 3), ("rs", 0, 2),
    ("rs", 4, 2), ("rs", 2, 2), ("rs", 3, 1), ("rs", 6, 2), ("start", 1), ("od",), ("rs", 0, 3), ("rs", 4, 3),
    ("tout",), ("rs", 2, 3), ("rs", 0, 4), ("rs", 6, 3), ("rs", 1, 1), ("rs", 3, 2), ("start", 5), ("rs", 4, 4),
    ("rs", 2, 4), ("rs", 5, 1), ("rs", 3, 3), ("rs", 1, 2), ("tmid",), ("mdown",), ("rs", 6, 4), ("pass", 0),
    ("pass", 4), ("gend",), ("rs", 5, 2), ("pass", 2), ("tend",), ("rs", 3, 4), ("rs", 1, 3), ("hid", 0), ("pass", 6),
    ("hid", 4), ("rs", 5, 3), ("hid", 2), ("rs", 1, 4), ("hid", 3), ("ag", 0, 2), ("ag", 4, 2), ("hid", 6),
    ("ag", 2, 2), ("rs", 5, 4), ("hid", 1), ("ag", 3, 1), ("ag", 4, 3), ("ag", 0, 3), ("ag", 6, 1), ("ag", 2, 3),
    ("hid", 5), ("ag", 1, 1), ("ag", 3, 2), ("ag", 4, 4), ("ag", 0, 4), ("ag", 6, 2), ("ag", 5, 1), ("ag", 1, 2),
    ("ag", 2, 4), ("down", 0), ("ag", 3, 3), ("ag", 4, 5), ("ag", 5, 2), ("ag", 1, 3), ("ag", 6, 3), ("down", 1),
    ("ag", 2, 5), ("ag", 5, 3), ("ag", 0, 5), ("ag", 3, 4), ("ag", 1, 4), ("down", 2), ("ag", 6, 4), ("ag", 5, 4),
    ("down", 3), ("ag", 1, 5), ("ag", 3, 5), ("ag", 6, 5), ("ag", 5, 5), ("down", 4),
)
T00 = (((0,), (0,)), ((), ()))
T11 = (((1,), (1,)), ((), ()))


def dot(a, b, dims=(((1,), (0,)), ((), ()))):
    return lax.dot_general(a, b, dims, preferred_element_type=F32)


def kernel(
    pick_ref, order_ref, tokens_ref, gi_hbm, ui_hbm, di_hbm, go_hbm, uo_hbm, do_hbm, gate_hbm, up_hbm, down_hbm, out_ref,
    gi, ui, di, go, uo, do,
    wg, wu, wd, x, ibuf, ogu, od, im, tsend, trec, tall, tbig, part, yrec_a, zrec_a, zrec_b, yrec_b, hid, obuf, orec,
    load_sem, x_sem, i_sem, o_sem, t_sem, gather_send,
    rsz_recv, rsy_recv, agz_recv, agy_recv, ring_send, out_sem, out_recv,
):
    row, col = lax.axis_index("row"), lax.axis_index("col")
    yh, z = row // 8, row % 8
    chip, core = col // 2, col % 2
    zat = lambda k: (z + k + 8) % 8
    up_dev = (yh * 8 + zat(1), col)
    down_dev = (yh * 8 + zat(-1), col)
    y_dev = ((1 - yh) * 8 + z, col)
    sib_dev = (row, chip * 2 + 1 - core)
    ring_dev = (up_dev, down_dev)

    def remote(src, dst, send, recv, dev):
        return pltpu.make_async_remote_copy(src, dst, send, recv, device_id=dev, device_id_type=MESH)

    def wait_recv(dst, recv):
        remote(dst, dst, gather_send.at[0], recv, y_dev).wait_recv()

    def wait_send(src, send):
        remote(src, src, send, out_sem.at[1], y_dev).wait_send()

    pools = ((go_hbm, go), (uo_hbm, uo), (gi_hbm, gi), (ui_hbm, ui), (di_hbm, di), (do_hbm, do))
    weights = ((gate_hbm, wg), (up_hbm, wu), (down_hbm, wd))
    loads = [pltpu.make_async_copy(src, dst, load_sem.at[i]) for i, (src, dst) in enumerate(pools + weights)]
    for load in loads:
        load.start()

    barrier = pltpu.get_barrier_semaphore()
    for k in range(1, 16):
        pl.semaphore_signal(barrier, inc=1, device_id=(row, (col + k) % 16), device_id_type=MESH)
    for k in range(1, 16):
        pl.semaphore_signal(barrier, inc=1, device_id=((row + k) % 16, col), device_id_type=MESH)

    def g_at(r):
        return ogu.at[pl.ds(pl.multiple_of(r * 112, 16), 112)]

    def d_at(r):
        return od.at[r]

    def x_at(chip_, core_):
        return x.at[pl.ds(core_ * 4, 4), pl.ds(pl.multiple_of(chip_ * 16, 16), 16)]

    k = pick_ref[0]
    r128 = lax.broadcasted_iota(jnp.int32, (64, 128), 0)
    c128 = lax.broadcasted_iota(jnp.int32, (64, 128), 1)
    left = jnp.where(r128 == c128, 1.0, 0.0).astype(BF)
    right = jnp.where(r128 + 64 == c128, 1.0, 0.0).astype(BF)
    one_hot = jnp.where(lax.broadcasted_iota(jnp.int32, (64, 64), 0) == order_ref[...] % 64, 1.0, 0.0).astype(BF)
    x_at(chip, core)[...] = dot(one_hot, tokens_ref[...], T00).astype(BF).reshape(4, 16, 512)
    loads[0].wait()
    loads[1].wait()
    g_at(row)[...] = (dot(go[k], left, T00) + dot(uo[k], right, T00)).astype(BF)
    loads[2].wait()
    loads[3].wait()
    ibuf[col, 0] = (dot(gi[k], left) + dot(ui[k], right)).astype(BF)
    loads[4].wait()
    loads[5].wait()
    ibuf[col, 1] = (dot(do[k], left) + dot(do[k], right)).astype(BF)
    low, high = dot(di[k], left, T00), dot(di[k], right, T00)[64:112]
    od[row] = (low[0:64] + jnp.concatenate([high, jnp.zeros((16, 128), F32)], axis=0)).astype(BF)
    pl.semaphore_wait(barrier, 30)

    far = (4, 3, 5, 2, 6, 1, 7)
    near = (1, 7, 2, 6, 3, 5, 4)

    def z_send(n, at):
        here = at(row)
        for k in far:
            remote(here, here, gather_send.at[2 + n], o_sem.at[n, 0, k], (yh * 8 + zat(k), col)).start()
        remote(here, here, gather_send.at[2 + n], o_sem.at[n, 1, 0], y_dev).start()

    def col_send(here, n, sem):
        for k in near:
            remote(here, here, gather_send.at[n], sem.at[0, k], (row, (chip + k) % 8 * 2 + core)).start()
        remote(here, here, gather_send.at[n], sem.at[1, 0], sib_dev).start()

    def z_pass(n, at):
        for k in near:
            here = at(yh * 8 + zat(-k))
            wait_recv(here, o_sem.at[n, 0, k])
            remote(here, here, gather_send.at[2 + n], o_sem.at[n, 1, k], y_dev).start()

    def z_end(n, at):
        for k in range(8):
            wait_recv(at((1 - yh) * 8 + zat(-k)), o_sem.at[n, 1, k])

    def col_pass(at, n, sem):
        for k in near:
            here = at((chip + 8 - k) % 8, core)
            wait_recv(here, sem.at[0, k])
            remote(here, here, gather_send.at[n], sem.at[1, k], sib_dev).start()

    def col_end(at, n, sem):
        for k in range(8):
            wait_recv(at((chip + 8 - k) % 8, 1 - core), sem.at[1, k])

    i_at = lambda chip_, core_: ibuf.at[chip_ * 2 + core_]
    col_send(x_at(chip, core), 0, x_sem)
    z_send(0, g_at)
    col_send(i_at(chip, core), 1, i_sem)
    z_send(1, d_at)
    col_pass(x_at, 0, x_sem)
    loads[6].wait()
    loads[7].wait()
    col_end(x_at, 0, x_sem)

    t_role = (yh == col // 8) & (z // 4 == core)
    t_from = lambda j: yh * 8 + j * 2 + z // 4

    def t_out():
        col_end(i_at, 1, i_sem)
        lane = lax.broadcasted_iota(jnp.int32, (512, 128), 1)
        im[0] = ibuf[:, 0].reshape(512, 128)
        narrow = ibuf[:, 1].reshape(512, 128)
        im[1] = jnp.where(lane < 64, narrow, jnp.zeros_like(narrow))
        im[2] = jnp.where(lane >= 64, narrow, jnp.zeros_like(narrow))
        tsend[...] = dot(x_at(chip, core)[...].reshape(64, 512), im[0]).reshape(4, 16, 128)
        for p in range(4):
            to = col // 8 * 8 + core * 4 + p

            @pl.when(to != row)
            def _():
                remote(tsend.at[p], trec.at[(to + 15 - row) % 16], t_sem.at[0], t_sem.at[1], (to, col)).start()

    def t_mid():
        @pl.when(t_role)
        def _():
            wait_recv(trec, t_sem.at[1])
            total = tsend[z % 4]
            for k in range(15):
                total = total + trec[k]
            mine = tall.at[chip % 4]
            mine[...] = total.astype(BF)
            for k in range(1, 16):
                remote(mine, mine, t_sem.at[2], t_sem.at[3 + chip % 4], (row, (col + k) % 16)).start()

    def t_end():
        for j in range(4):
            @pl.when(t_from(j) != col)
            def _():
                wait_recv(tall.at[j], t_sem.at[3 + j])

    def merge_down():
        z_end(1, d_at)
        loads[8].wait()

        @pl.loop(0, 16)
        def _(r):
            for first, size, n in ((0, 64, 1), (64, 48, 2)):
                at = pl.ds(pl.multiple_of(r * 112 + first, 16), size)
                low = dot(od[r, 0:size], im[n], T11)
                wd[at] = (wd[at].astype(F32) + 2.0 * low).astype(BF)

    def products(g):
        cols = slice(g * GW, (g + 1) * GW)

        @pl.loop(0, 2)
        def _(i):
            rows = x[pl.ds(i * 4, 4)].reshape(512, 512)
            for half, w in enumerate((wg, wu)):
                term = dot(rows, w[:, cols])
                part[g, pl.ds(i * 4, 4), :, :, half * GW:(half + 1) * GW] = term.astype(BF).reshape(4, 2, 64, GW)

    def rs_refs(g):
        if g in A_GROUPS:
            n = A_GROUPS.index(g)
            return zrec_a.at[n], (lambda d: part.at[g, d, yh]), yrec_a.at[n]
        n = B_GROUPS.index(g)
        return zrec_b.at[n], (lambda d: part.at[g, d]), None

    def lanes(half):
        return pl.ds(half * GW, GW)

    def rs_y(g):
        _, _, yrec = rs_refs(g)
        for k in (4, 3, 5, 2, 6, 1, 7, 0):
            d = zat(k)
            remote(part.at[g, d, 1 - yh], yrec.at[d], ring_send.at[1, g], rsy_recv.at[g, k], y_dev).start()

    def y_wait(g, k):
        _, _, yrec = rs_refs(g)
        wait_recv(yrec.at[zat(k)], rsy_recv.at[g, k])

    def rs_1(g):
        zrec, at, yrec = rs_refs(g)
        d = zat(4)
        if yrec is not None:
            y_wait(g, 4)
            at(d)[...] = (at(d)[...].astype(F32) + yrec[d].astype(F32)).astype(BF)
        for way in (CW, CCW):
            remote(
                at(d).at[..., lanes(way)], zrec.at[way, 0].at[..., lanes(way)],
                ring_send.at[0, g], rsz_recv.at[g, way, 0], ring_dev[way],
            ).start()

    def rs_s(g, s):
        zrec, at, yrec = rs_refs(g)
        for way in (CW, CCW):
            d = zat(5 - s if way == CW else s - 5)
            if yrec is not None:
                y_wait(g, 5 - s if way == CW else s + 3)
            got = zrec.at[way, s - 2]
            spot = at(d)
            if s == 2:
                wait_recv(got.at[..., lanes(way)], rsz_recv.at[g, way, 0])
                for half in (0, 1):
                    total = spot[..., lanes(half)].astype(F32)
                    if yrec is not None:
                        total = total + yrec[d, :, lanes(half)].astype(F32)
                    if half == way:
                        total = total + got[..., lanes(half)].astype(F32)
                    if half == way or yrec is not None:
                        spot[..., lanes(half)] = total.astype(BF)
            else:
                wait_recv(got, rsz_recv.at[g, way, s - 2])
                total = spot[...].astype(F32) + got[...].astype(F32)
                if yrec is not None:
                    total = total + yrec[d].astype(F32)
                spot[...] = total.astype(BF)
            remote(spot, zrec.at[way, s - 1], ring_send.at[0, g], rsz_recv.at[g, way, s - 1], ring_dev[way]).start()

    def rs_end(g):
        zrec, at, _ = rs_refs(g)
        for way in (CW, CCW):
            wait_recv(zrec.at[way, 3], rsz_recv.at[g, way, 3])

    def rs_pass(g):
        rs_end(g)
        zrec, at, _ = rs_refs(g)
        away = part.at[g, z, 1 - yh]
        total = away[...].astype(F32) + zrec[CW, 3, 1 - yh].astype(F32) + zrec[CCW, 3, 1 - yh].astype(F32)
        away[...] = total.astype(BF)
        remote(away, yrec_b.at[B_GROUPS.index(g)], ring_send.at[1, g], rsy_recv.at[g, 0], y_dev).start()

    def hidden(g):
        if g in A_GROUPS:
            rs_end(g)
            y_wait(g, 0)
            zrec, at, yrec = rs_refs(g)
            terms = (part.at[g, z, yh], yrec.at[z], zrec.at[CW, 3], zrec.at[CCW, 3])
        else:
            n = B_GROUPS.index(g)
            wait_recv(yrec_b.at[n], rsy_recv.at[g, 0])
            terms = (part.at[g, z, yh], zrec_b.at[n, CW, 3, yh], zrec_b.at[n, CCW, 3, yh], yrec_b.at[n])
        sums = []
        pair = tall[...].reshape(64, 128)
        lane = lax.broadcasted_iota(jnp.int32, (64, 128), 1)
        for half in (0, 1):
            total = terms[0][:, lanes(half)].astype(F32)
            for term in terms[1:]:
                total = total + term[:, lanes(half)].astype(F32)
            one = jnp.where((lane < 64) if half == 0 else (lane >= 64), pair, jnp.zeros_like(pair))
            sums.append(total + 2.0 * dot(one, ogu[g * GW:(g + 1) * GW], T11))
        gate, up = sums
        hid[z, yh, :, g * GW:(g + 1) * GW] = (gate / (1.0 + jnp.exp(-gate)) * up).astype(BF)
        ag_y(g, 0)
        if g in AGY:
            ag_z(g)

    def h_at(g, d, s=1, way=None):
        lo, n = (g * GW, GW) if s < 4 else (g * GW + way * GW // 2, GW // 2)
        if g in AGY:
            return hid.at[d, yh, :, pl.ds(lo, n)]
        return hid.at[d, :, :, pl.ds(lo, n)]

    def ag_y(g, k):
        ref = hid.at[zat(k), yh, :, pl.ds(g * GW, GW)]
        remote(ref, ref, ring_send.at[3, g], agy_recv.at[g, k % 8], y_dev).start()

    def ag_z(g):
        for way in (CW, CCW):
            ref = h_at(g, z)
            remote(ref, ref, ring_send.at[2, g], agz_recv.at[g, way, 0], ring_dev[way]).start()

    def ag_y_wait(g, k):
        wait_recv(hid.at[zat(k), 1 - yh, :, pl.ds(g * GW, GW)], agy_recv.at[g, k % 8])

    def ag_1(g):
        ag_y_wait(g, 0)
        ag_z(g)

    def ag_s(g, s):
        for way in (CW, CCW):
            d = zat(1 - s if way == CW else s - 1)
            wait_recv(h_at(g, d), agz_recv.at[g, way, s - 2])
            ref = h_at(g, d, s, way)
            remote(ref, ref, ring_send.at[2, g], agz_recv.at[g, way, s - 1], ring_dev[way]).start()
            if g in AGY:
                ag_y(g, 1 - s if way == CW else s - 1)

    def ag_end(g):
        for way in (CW, CCW):
            wait_recv(h_at(g, zat(4), 4, way), agz_recv.at[g, way, 3])
        if g in AGY:
            ag_y(g, 4)

    def down(*offsets):
        places = [zat(k) for k in offsets]
        n = len(places)
        for g in AGY:
            for k in offsets:
                ag_y_wait(g, k)
        rows = [hid[d].reshape(128, GROUPS * GW) for d in places]
        term = dot(rows[0] if n == 1 else jnp.concatenate(rows, axis=0), wd[...])
        for m, d in enumerate(places):
            obuf[d] = term[m * 128:(m + 1) * 128].astype(BF).reshape(8, 16, 512)
        for d in places:
            @pl.loop(0, 8)
            def _(j):
                to = j * 2 + d // 4

                @pl.when(to != col)
                def _():
                    remote(
                        obuf.at[d, j], orec.at[(to + 15 - col) % 16, d % 4],
                        out_sem.at[0], out_recv.at[d % 4], (row, to),
                    ).start()

    def start(g):
        products(g)
        if g in A_GROUPS:
            rs_y(g)
        else:
            rs_1(g)

    def rs(g, s):
        rs_1(g) if s == 1 else rs_s(g, s)

    def ag(g, s):
        ag_1(g) if s == 1 else ag_end(g) if s == 5 else ag_s(g, s)

    def rows_done(k):
        down(*((k,) if k in (0, 4) else (k, -k)))

    tasks = {
        "start": start, "rs": rs, "pass": rs_pass, "hid": hidden, "ag": ag,
        "ipass": lambda: col_pass(i_at, 1, i_sem), "gpass": lambda: z_pass(0, g_at), "gend": lambda: z_end(0, g_at),
        "tout": t_out, "tmid": t_mid, "tend": t_end,
        "od": lambda: z_pass(1, d_at), "mdown": merge_down, "down": rows_done,
    }
    for name, *rest in ORDER:
        tasks[name](*rest)

    for k in (0, 1, 7, 2, 6, 3, 5, 4):
        d = zat(k)
        p = d % 4

        @pl.when(d // 4 == core)
        def _():
            wait_recv(orec.at[:, p], out_recv.at[p])
            total = obuf[d, chip].astype(F32)
            for n in range(15):
                total = total + orec[n, p].astype(F32)
            out_ref[p] = total.astype(BF)

    wait_send(orec, out_sem.at[0])
    wait_send(orec, gather_send.at[0])
    wait_send(ibuf.at[pl.ds(0, 15)], gather_send.at[1])
    wait_send(ogu.at[pl.ds(0, 15 * 112)], gather_send.at[2])
    wait_send(od.at[pl.ds(0, 15)], gather_send.at[3])
    sent = col // 8 * 8 + core * 4

    @pl.when((row >= sent) & (row < sent + 4))
    def _():
        wait_send(tsend.at[pl.ds(0, 3)], t_sem.at[0])

    @pl.when((row < sent) | (row >= sent + 4))
    def _():
        wait_send(tsend, t_sem.at[0])

    @pl.when(t_role)
    def _():
        wait_send(tbig, t_sem.at[2])

    for g in range(GROUPS):
        cols = pl.ds(g * GW, GW)
        if g in A_GROUPS:
            wait_send(part.at[g, pl.ds(0, 7), 0], ring_send.at[0, g])
            wait_send(part.at[g, :, 0], ring_send.at[1, g])
        else:
            wait_send(part.at[g, pl.ds(0, 7)], ring_send.at[0, g])
            wait_send(part.at[g, 0, 0], ring_send.at[1, g])
        if g in AGY:
            wait_send(hid.at[pl.ds(0, 7), 0, :, cols], ring_send.at[2, g])
            wait_send(hid.at[:, 0, :, cols], ring_send.at[3, g])
        else:
            wait_send(hid.at[pl.ds(0, 7), :, :, cols], ring_send.at[2, g])
            wait_send(hid.at[0, 0, :, cols], ring_send.at[3, g])


def layer(pick, order, tokens, *arrays):
    vmem = pl.BlockSpec(memory_space=pltpu.VMEM)
    hbm = pl.BlockSpec(memory_space=pl.ANY)
    smem = pl.BlockSpec(memory_space=pltpu.SMEM)
    dma = pltpu.SemaphoreType.DMA
    return pl.pallas_call(
        kernel,
        out_shape=jax.ShapeDtypeStruct((4, 16, 512), BF),
        in_specs=[smem, vmem, vmem] + [hbm] * 9,
        out_specs=vmem,
        scratch_shapes=[pltpu.VMEM(a.shape, BF) for a in arrays[:6]] + [
            pltpu.VMEM((512, 1792), BF),
            pltpu.VMEM((512, 1792), BF),
            pltpu.VMEM((1792, 512), BF),
            pltpu.VMEM((8, 128, 512), BF),
            pltpu.VMEM((16, 2, 32, 128), BF),
            pltpu.VMEM((1792, 128), BF),
            pltpu.VMEM((16, 64, 128), BF),
            pltpu.VMEM((3, 512, 128), BF),
            pltpu.VMEM((4, 16, 128), F32),
            pltpu.VMEM((15, 16, 128), F32),
            pltpu.VMEM((4, 16, 128), BF),
            pltpu.VMEM((15, 16, 128), BF),
            pltpu.VMEM((GROUPS, 8, 2, 64, 2 * GW), BF),
            pltpu.VMEM((NA, 8, 64, 2 * GW), BF),
            pltpu.VMEM((NA, 2, 4, 64, 2 * GW), BF),
            pltpu.VMEM((NB, 2, 4, 2, 64, 2 * GW), BF),
            pltpu.VMEM((NB, 64, 2 * GW), BF),
            pltpu.VMEM((8, 2, 64, GROUPS * GW), BF),
            pltpu.VMEM((8, 8, 16, 512), BF),
            pltpu.VMEM((15, 4, 16, 512), BF),
            dma((9,)),
            dma((2, 8)),
            dma((2, 8)),
            dma((2, 2, 8)),
            dma((7,)),
            dma((4,)),
            dma((GROUPS, 2, 4)),
            dma((GROUPS, 8)),
            dma((GROUPS, 2, 4)),
            dma((GROUPS, 8)),
            dma((4, GROUPS)),
            dma((2,)),
            dma((4,)),
        ],
        compiler_params=pltpu.CompilerParams(
            collective_id=0, has_side_effects=True, vmem_limit_bytes=56 * 2**20
        ),
    )(pick, order, tokens, *arrays)


def body(
    tokens, row_order, adapter_id, gate_weight, up_weight, down_weight,
    gate_inner, gate_outer, up_inner, up_outer, down_inner, down_outer,
):
    swap = lambda a: jnp.swapaxes(a, 1, 2)
    return layer(
        adapter_id, row_order.reshape(1, 64), tokens,
        gate_inner, up_inner, swap(down_inner), gate_outer, up_outer, swap(down_outer),
        gate_weight, up_weight, down_weight,
    ).reshape(64, 512)


def solution(mesh):
    return jax.shard_map(
        body,
        mesh=mesh,
        in_specs=(
            P("col", "row"),
            P("col"),
            P(),
            P("row", "col"),
            P("row", "col"),
            P("col", "row"),
            P(None, ("row", "col"), None),
            P(None, None, ("col", "row")),
            P(None, ("row", "col"), None),
            P(None, None, ("col", "row")),
            P(None, ("col", "row"), None),
            P(None, None, ("row", "col")),
        ),
        out_specs=P("col", "row"),
        check_vma=False,
    )
```
